128 devices in a mesh: snap: 8 (over x, core), dof: 16 (over z, y).
Axes of the slice: x: 4, y: 4, z: 4, core: 2. Of those that a mesh axis runs over, the one named last changes fastest.
Arguments:
- snapshots: float32 [256, 524288], P('snap', 'dof'), may hold values from -12 to 12
- picks: int32 [3, 32], replicated, may hold values from 0 to 255, as said below
Outputs:
- basis: float32 [96, 524288], P(None, 'dof')
- residual: float32 [256, 524288], P('snap', 'dof')
The draws below stay inside these ranges and needn't reach their ends.
Inputs may be any that keep to these rules, and one draw needn't show every extreme that they name: `picks`: within a step the 32 indices are distinct, and no index appears at two steps. At each step at most 8 indices fall among the 32 snapshots of one index of snap, and exactly 8 in at least one of them.
All inputs are finite; a program needn't handle non-finite values.
Results may differ from the reference program's by a relative error of at most 0.0003.
Values sent between devices are 32-bit elements; how exact they have to be, the bound alone decides.
A program may use at most 128 MiB of HBM per device.

```python
import jax
import jax.numpy as jnp
from jax import lax

SNAP_DEV = 32
K = 32
STEPS = 3
MOST = 8
NDOF = 524288
NSNAP = 256


def draw_snapshots(key, part):
    key = jax.random.fold_in(key, 5)
    row_scale = jnp.power(10.0, jax.random.uniform(jax.random.fold_in(key, 1), (1, NDOF), jnp.float32) - 0.5)
    col_scale = jnp.exp(jax.random.uniform(jax.random.fold_in(key, 2), (NSNAP, 1), jnp.float32, -0.7, 0.7))
    modes = jax.random.normal(jax.random.fold_in(key, 3), (4, 1, NDOF), jnp.float32)
    loads = jax.random.normal(jax.random.fold_in(key, 4), (4, NSNAP, 1), jnp.float32)
    common = modes[0] * loads[0] + modes[1] * loads[1] + modes[2] * loads[2] + modes[3] * loads[3]
    noise = jax.random.normal(jax.random.fold_in(key, 6), (NSNAP, NDOF), jnp.float32)
    mixed = common + 0.5 * noise * row_scale
    return jnp.clip(mixed * col_scale, -12.0, 12.0).astype(jnp.float32)


def draw_picks(key, part):
    key = jax.random.fold_in(key, 11)
    groups = NSNAP // SNAP_DEV
    group_keys = jax.random.split(jax.random.fold_in(key, 1), groups)
    local_order = jax.vmap(lambda group_key: jax.random.permutation(group_key, SNAP_DEV))(group_keys)
    slot_count = groups * MOST
    slot_group = jnp.arange(slot_count, dtype=jnp.int32) // MOST
    slot_rank = jnp.arange(slot_count, dtype=jnp.int32) % MOST
    rows_out = []
    for step_index in range(STEPS):
        step_key = jax.random.fold_in(key, 100 + step_index)
        full_group = jax.random.randint(jax.random.fold_in(step_key, 1), (), 0, groups)
        order_score = jax.random.permutation(jax.random.fold_in(step_key, 2), slot_count).astype(jnp.int32)
        score = order_score + jnp.where(slot_group == full_group, 0, slot_count).astype(jnp.int32)
        chosen = jnp.argsort(score, stable=True)[:K]
        chosen_group = slot_group[chosen]
        chosen_rank = slot_rank[chosen]
        local_pos = local_order[chosen_group, step_index * MOST + chosen_rank]
        rows_out.append(chosen_group * SNAP_DEV + local_pos)
    return jnp.stack(rows_out).astype(jnp.int32)


def setup_inputs(seed: int = 0) -> dict:
    key_list = jax.random.split(jax.random.key(seed), 3)
    snapshots = draw_snapshots(jax.random.fold_in(key_list[2], 71), 0)
    picks = draw_picks(jax.random.fold_in(key_list[2], 71), 0)
    return dict(snapshots=snapshots, picks=picks)


def matmul(left, right):
    return jnp.dot(left.astype(jnp.float32), right.astype(jnp.float32), precision=lax.Precision.HIGHEST, preferred_element_type=jnp.float32)

def inner_product(left, right):
    return lax.dot_general(left.astype(jnp.float32), right.astype(jnp.float32), (((1,), (1,)), ((), ())), precision=lax.Precision.HIGHEST, preferred_element_type=jnp.float32)

def inverse_factor(gram_mat):
    lower_factor = jnp.linalg.cholesky(gram_mat)
    return jax.scipy.linalg.solve_triangular(lower_factor, jnp.eye(gram_mat.shape[0], dtype=jnp.float32), lower=True)

def reference(snapshots, picks):
    inverse_count = 1.0 / NDOF
    residual = snapshots
    basis = jnp.zeros((0, NDOF), jnp.float32)
    for step_index in range(STEPS):
        picked = jnp.take(snapshots, picks[step_index].astype(jnp.int32), axis=0)
        if step_index > 0:
            correlation = inner_product(basis, picked) * inverse_count
            picked = picked - matmul(correlation.T, basis)
        gram_mat = inner_product(picked, picked) * inverse_count
        factor_inv = inverse_factor(gram_mat)
        new_basis = matmul(factor_inv, picked)
        coefficients = inner_product(new_basis, residual) * inverse_count
        residual = residual - matmul(coefficients.T, new_basis)
        basis = jnp.concatenate([basis, new_basis], axis=0)
    return (basis, residual)
```

```python
import functools

import jax
import jax.numpy as jnp
from jax import lax
from jax.experimental import pallas as pl
from jax.experimental.pallas import tpu as pltpu
from jax.sharding import PartitionSpec as P

F32 = jnp.float32
BF16 = jnp.bfloat16
MESH = pl.DeviceIdType.MESH
RING = 4
CORES = 2
PIECES = 4
LAG = 2
TX = 4
SEMS = 8


def iota(shape, dim):
    return lax.broadcasted_iota(jnp.int32, shape, dim).astype(F32)


def split(value, parts):
    out = []
    for index in range(parts):
        part = value.astype(BF16)
        out.append(part)
        if index < parts - 1:
            value = value - part.astype(F32)
    return out


def choose(one_hot, rows):
    total = None
    for part in split(rows, 3):
        term = jnp.dot(one_hot, part, preferred_element_type=F32)
        total = term if total is None else total + term
    return total


def plan(picks, cap, x, core):
    steps, block = picks.shape
    count = steps * block
    rows_chip = 64
    eye = iota((block, block), 0) == iota((block, block), 1)
    columns = [
        jnp.sum(jnp.where(eye, jnp.broadcast_to(picks[t : t + 1, :], (block, block)), 0.0), axis=1, keepdims=True)
        for t in range(steps)
    ]
    pick = jnp.concatenate(columns, axis=0)
    owner = jnp.floor(pick * (1.0 / rows_chip))
    row = pick - owner * rows_chip
    row = jnp.where(row < 32.0, row + 32.0 * core, row - 32.0 * core)
    big_eye = iota((count, count), 0) == iota((count, count), 1)

    def across(column):
        return jnp.sum(jnp.where(big_eye, jnp.broadcast_to(column, (count, count)), 0.0), axis=0, keepdims=True)

    owner_across = across(owner)
    earlier = iota((count, count), 1) < iota((count, count), 0)
    same = jnp.broadcast_to(owner_across, (count, count)) == jnp.broadcast_to(owner, (count, count))
    rank = jnp.sum(jnp.where(same & earlier, 1.0, 0.0), axis=1, keepdims=True)

    before = lax.rem(x + RING - 1, RING).astype(F32)
    here = x.astype(F32)
    after = lax.rem(x + 1, RING).astype(F32)
    across_ring = lax.rem(x + 2, RING).astype(F32)

    def owned(chip):
        return jnp.sum(jnp.where(owner == chip, 1.0, 0.0), axis=0, keepdims=True)

    own_before, own_here, own_after, own_across = owned(before), owned(here), owned(after), owned(across_ring)
    up_before = jnp.clip(cap - own_here, 0.0, own_before)
    up_after = jnp.clip(cap - own_across, 0.0, own_after)
    up_across = jnp.clip(cap - own_before, 0.0, own_across)

    place = jnp.where(owner == here, row, 0.0)
    place = jnp.where(owner == before, 64.0 + rank, place)
    place = jnp.where(owner == after, 64.0 + cap + rank, place)
    far = jnp.where(
        rank < up_across,
        64.0 + 2 * cap + own_before + rank,
        64.0 + 3 * cap + own_after + rank - up_across,
    )
    place = jnp.where(owner == across_ring, far, place)
    width = 64 + 4 * cap
    collect = jnp.where(iota((count, width), 1) == place, 1.0, 0.0).astype(BF16)

    slot = iota((cap, 1), 0)
    rank_across, row_across = across(rank), across(row)
    hit = (jnp.broadcast_to(rank_across, (cap, count)) == iota((cap, count), 0)) & (
        jnp.broadcast_to(owner_across, (cap, count)) == here
    )
    own_row = jnp.sum(jnp.where(hit, jnp.broadcast_to(row_across, (cap, count)), 0.0), axis=1, keepdims=True)
    extra = slot - own_here
    up = jnp.where(extra < up_before, 64.0 + extra, -1.0)
    down = jnp.where(extra < own_after - up_after, 64.0 + cap + up_after + extra, -1.0)
    mine = slot < own_here
    source = jnp.concatenate([jnp.where(mine, own_row, up), jnp.where(mine, own_row, down)], axis=0)
    send = jnp.where(iota((2 * cap, 64 + 2 * cap), 1) == source, 1.0, 0.0).astype(BF16)
    return send, collect


def gather_kernel(
    cap, chunks, width,
    snap_ref, picks_ref, rows_ref, sums_ref,
    local, other, inbox, outbox, rows, send_hot, collect_hot, total, ybuf, zbuf,
    load_sem, swap_send, swap_recv, out_send, in_recv, pass_send, pass_recv, store_sem, sum_send, sum_recv,
):
    half = chunks * width
    snap, dof = lax.axis_index("snap"), lax.axis_index("dof")
    x, core = lax.div(snap, CORES), lax.rem(snap, CORES)
    z, y = lax.div(dof, RING), lax.rem(dof, RING)
    sibling = (x * CORES + 1 - core, dof)
    up = (lax.rem(x + 1, RING) * CORES + core, dof)
    down = (lax.rem(x + RING - 1, RING) * CORES + core, dof)
    along_y = [(snap, z * RING + lax.rem(y + k, RING)) for k in range(1, RING)]
    along_z = [(snap, lax.rem(z + k, RING) * RING + y) for k in range(1, RING)]
    peers = [sibling, up, down] + along_y + along_z

    barrier = pltpu.get_barrier_semaphore()
    for peer in peers:
        pl.semaphore_signal(barrier, inc=1, device_id=peer, device_id_type=MESH)

    piece = half // PIECES
    mine = pl.multiple_of(core * half, half)
    theirs = pl.multiple_of((1 - core) * half, half)

    def load(index):
        start = pl.multiple_of(mine + index * piece, piece) if index < PIECES else theirs
        size = piece if index < PIECES else half
        where = (slice(None), pl.ds(start, size))
        return pltpu.make_async_copy(snap_ref.at[where], local.at[where], load_sem.at[index])

    def swap(index):
        start = pl.multiple_of(theirs + index * piece, piece)
        return pltpu.make_async_remote_copy(
            src_ref=snap_ref.at[:, pl.ds(start, piece)],
            dst_ref=other.at[:, pl.ds(index * piece, piece)],
            send_sem=swap_send.at[index],
            recv_sem=swap_recv.at[index],
            device_id=sibling,
            device_id_type=MESH,
        )

    for index in range(PIECES + 1):
        load(index).start()
    send, collect = plan(picks_ref[...].astype(F32), cap, x, core)
    send_hot[...] = send
    collect_hot[...] = collect
    total[...] = jnp.zeros_like(total)
    for way in range(2):
        for slot in range(LAG):
            inbox[way, slot] = jnp.zeros((cap, width), F32)
    pl.semaphore_wait(barrier, len(peers))
    for index in range(PIECES):
        swap(index).start()

    def message(step, way):
        return pltpu.make_async_remote_copy(
            src_ref=outbox.at[lax.rem(step, TX), way],
            dst_ref=inbox.at[way, step + LAG],
            send_sem=out_send.at[way, lax.rem(step, TX)],
            recv_sem=in_recv.at[way, lax.rem(step, SEMS)],
            device_id=up if way == 0 else down,
            device_id_type=MESH,
        )

    def hand_over(chunk):
        return pltpu.make_async_remote_copy(
            src_ref=rows.at[core, chunk],
            dst_ref=rows.at[core, chunk],
            send_sem=pass_send.at[lax.rem(chunk, SEMS)],
            recv_sem=pass_recv.at[chunk],
            device_id=sibling,
            device_id_type=MESH,
        )

    def store(which, chunk, sem_row):
        return pltpu.make_async_copy(
            rows.at[which, chunk], rows_ref.at[which, chunk], store_sem.at[sem_row, lax.rem(chunk, SEMS)]
        )

    def local_chunk(base, chunk):
        return local[:, pl.ds(pl.multiple_of(base + chunk * width, width), width)]

    def other_chunk(chunk):
        return other[:, pl.ds(pl.multiple_of(chunk * width, width), width)]

    def add_products(which, picked, snaps):
        picked_parts, snap_parts = split(picked, 2), split(snaps, 2)
        left = jnp.concatenate(picked_parts, axis=0)
        right = jnp.concatenate([picked_parts[0], snap_parts[0], picked_parts[1], snap_parts[1]], axis=0)
        total[which] += lax.dot_general(left, right, (((1,), (1,)), ((), ())), preferred_element_type=F32)

    def body(step, carry):
        for index in range(PIECES):
            @pl.when(step == index * (chunks // PIECES))
            def _():
                load(index).wait()
                swap(index).wait()

        @pl.when(step == LAG)
        def _():
            load(PIECES).wait()

        @pl.when((step >= LAG) & (step < chunks + 2 * LAG))
        def _():
            for way in range(2):
                message(step - LAG, way).wait_recv()

        @pl.when(step < chunks + LAG)
        def _():
            @pl.when(step >= TX)
            def _():
                for way in range(2):
                    message(step - TX, way).wait_send()

            chunk = jnp.minimum(step, chunks - 1)
            stage = jnp.concatenate(
                [local_chunk(mine, chunk), other_chunk(chunk), inbox[0, step], inbox[1, step]], axis=0
            )
            sent = choose(send_hot[...], stage)
            slot = lax.rem(step, TX)
            outbox[slot, 0] = sent[:cap]
            outbox[slot, 1] = sent[cap:]
            for way in range(2):
                message(step, way).start()

        @pl.when((step >= 2 * LAG) & (step < chunks + 2 * LAG))
        def _():
            chunk = step - 2 * LAG
            here = local_chunk(mine, chunk)
            stage = jnp.concatenate(
                [here, other_chunk(chunk), inbox[0, step - LAG], inbox[1, step - LAG], inbox[0, step], inbox[1, step]],
                axis=0,
            )
            picked = choose(collect_hot[...], stage)
            rows[core, chunk] = picked

            @pl.when(chunk >= SEMS)
            def _():
                hand_over(chunk - SEMS).wait_send()
                store(core, chunk - SEMS, 0).wait()

            hand_over(chunk).start()
            store(core, chunk, 0).start()
            add_products(core, picked, here)

        @pl.when(step >= 2 * LAG + 1)
        def _():
            chunk = step - 2 * LAG - 1
            hand_over(chunk).wait_recv()

            @pl.when(chunk >= SEMS)
            def _():
                store(1 - core, chunk - SEMS, 1).wait()

            store(1 - core, chunk, 1).start()
            add_products(1 - core, rows[1 - core, chunk], local_chunk(theirs, chunk))

        return carry

    lax.fori_loop(0, chunks + 2 * LAG + 1, body, 0)

    both = total[0] + total[1]
    count = both.shape[0] // 2
    wide = both.shape[1] // 2
    sums = both[:count, :wide] + both[:count, wide:] + (both[count:, :wide] + both[count:, wide:])
    for stage, (buf, peers_here, me) in enumerate(((ybuf, along_y, y), (zbuf, along_z, z))):
        buf[me] = sums
        copies = [
            pltpu.make_async_remote_copy(
                src_ref=buf.at[me],
                dst_ref=buf.at[me],
                send_sem=sum_send.at[stage, k],
                recv_sem=sum_recv.at[stage, k],
                device_id=peer,
                device_id_type=MESH,
            )
            for k, peer in enumerate(peers_here)
        ]
        for copy in copies:
            copy.start()
        for copy in copies:
            copy.wait()
        sums = (buf[0] + buf[1]) + (buf[2] + buf[3])
    sums_ref[...] = sums * (1.0 / (2 * half * lax.axis_size("dof")))

    for step in range(chunks + LAG - TX, chunks + LAG):
        for way in range(2):
            message(step, way).wait_send()
    for chunk in range(chunks - SEMS, chunks):
        hand_over(chunk).wait_send()
        store(core, chunk, 0).wait()
        store(1 - core, chunk, 1).wait()


def gather(snapshots, picks, cap, chunks, collective_id):
    snap_rows, cols = snapshots.shape
    steps, block = picks.shape
    count = steps * block
    half = cols // 2
    width = half // chunks
    dma = pltpu.SemaphoreType.DMA
    return pl.pallas_call(
        functools.partial(gather_kernel, cap, chunks, width),
        name=f"gather_{cap}",
        out_shape=(
            jax.ShapeDtypeStruct((2, chunks, count, width), F32),
            jax.ShapeDtypeStruct((count, count + snap_rows), F32),
        ),
        in_specs=[pl.BlockSpec(memory_space=pl.ANY), pl.BlockSpec(memory_space=pltpu.VMEM)],
        out_specs=(pl.BlockSpec(memory_space=pl.ANY), pl.BlockSpec(memory_space=pltpu.VMEM)),
        scratch_shapes=[
            pltpu.VMEM((snap_rows, cols), F32),
            pltpu.VMEM((snap_rows, half), F32),
            pltpu.VMEM((2, chunks + 2 * LAG, cap, width), F32),
            pltpu.VMEM((TX, 2, cap, width), F32),
            pltpu.VMEM((2, chunks, count, width), F32),
            pltpu.VMEM((2 * cap, 64 + 2 * cap), BF16),
            pltpu.VMEM((count, 64 + 4 * cap), BF16),
            pltpu.VMEM((2, 2 * count, 2 * (count + snap_rows)), F32),
            pltpu.VMEM((RING, count, count + snap_rows), F32),
            pltpu.VMEM((RING, count, count + snap_rows), F32),
            dma((PIECES + 1,)),
            dma((PIECES,)),
            dma((PIECES,)),
            dma((2, TX)),
            dma((2, SEMS)),
            dma((SEMS,)),
            dma((chunks,)),
            dma((2, SEMS)),
            dma((2, RING - 1)),
            dma((2, RING - 1)),
        ],
        compiler_params=pltpu.CompilerParams(
            collective_id=collective_id, has_side_effects=True, vmem_limit_bytes=48 << 20
        ),
    )(snapshots, picks)


def eliminate(sums, count):
    tiles = count // 8
    lanes = sums.shape[1]
    left = [sums[8 * t : 8 * t + 8, :] for t in range(tiles)]
    right = [
        jnp.where(iota((8, lanes), 1) == iota((8, lanes), 0) + 8.0 * t, 1.0, 0.0) for t in range(tiles)
    ]
    sub = iota((8, lanes), 0)
    pivots = []
    for j in range(count):
        t0, r = divmod(j, 8)
        pivot_row = jnp.broadcast_to(left[t0][r : r + 1, :], (8, lanes))
        right_row = jnp.broadcast_to(right[t0][r : r + 1, :], (8, lanes))
        pivot = jnp.broadcast_to(pivot_row[:, j : j + 1], (8, lanes))
        pivots.append(pivot[:1, :])
        inverse = 1.0 / pivot
        pivot_row = pivot_row * inverse
        right_row = right_row * inverse
        for t in range(t0, tiles):
            factor = jnp.broadcast_to(left[t][:, j : j + 1], (8, lanes))
            if t == t0:
                factor = jnp.where(sub > r, factor, 0.0)
            left[t] = left[t] - factor * pivot_row
            right[t] = right[t] - factor * right_row
    return jnp.concatenate(left, axis=0), jnp.concatenate(right, axis=0), jnp.concatenate(pivots, axis=0)


def apply_kernel(
    chunks, width, rows_ref, sums_ref, snap_ref, basis_ref, residual_ref,
    rows, snaps, basis, residual, weights, rows_sem, snap_sem, basis_sem, residual_sem,
):
    count = basis.shape[0]
    group = 2 * chunks // PIECES

    def load_rows(index):
        where = pl.ds(index * group, group)
        return pltpu.make_async_copy(rows_ref.at[where], rows.at[where], rows_sem.at[index])

    for index in range(PIECES):
        load_rows(index).start()
    load_snaps = pltpu.make_async_copy(snap_ref, snaps, snap_sem)
    load_snaps.start()

    left, right, pivots = eliminate(sums_ref[...], count)
    inverse = right[:, :count]
    cross = left[:, count:]
    scale = lax.rsqrt(pivots[:, :1])
    to_basis = inverse * scale
    coefficients = cross * (1.0 / pivots[:, : cross.shape[1]])
    to_residual = lax.dot_general(
        coefficients, inverse, (((0,), (0,)), ((), ())),
        precision=lax.Precision.HIGHEST, preferred_element_type=F32,
    )
    high, low = split(jnp.concatenate([to_basis, to_residual], axis=0), 2)
    weights[...] = jnp.concatenate(
        [jnp.concatenate([high, high], axis=1), jnp.concatenate([low, low], axis=1)], axis=0
    )

    def put_basis(index):
        where = (slice(None), pl.ds(pl.multiple_of(index * width, width), width))
        return pltpu.make_async_copy(basis.at[where], basis_ref.at[where], basis_sem.at[lax.rem(index, SEMS)])

    def put_residual(index):
        where = (slice(None), pl.ds(pl.multiple_of(index * width, width), width))
        return pltpu.make_async_copy(
            residual.at[where], residual_ref.at[where], residual_sem.at[lax.rem(index, SEMS)]
        )

    load_snaps.wait()

    def body(index, carry):
        for piece in range(PIECES):
            @pl.when(index == piece * group)
            def _():
                load_rows(piece).wait()

        high, low = split(rows[index], 2)
        stack = jnp.concatenate([high, low], axis=0)
        out = jnp.dot(weights[...], stack, preferred_element_type=F32)
        out_rows = out.shape[0] // 2
        out = out[:out_rows] + out[out_rows:]
        where = (slice(None), pl.ds(pl.multiple_of(index * width, width), width))
        basis[where] = out[:count]
        residual[where] = snaps[where] - out[count:]

        @pl.when(index >= SEMS)
        def _():
            put_basis(index - SEMS).wait()
            put_residual(index - SEMS).wait()

        put_basis(index).start()
        put_residual(index).start()
        return carry

    lax.fori_loop(0, 2 * chunks, body, 0)
    for index in range(2 * chunks - SEMS, 2 * chunks):
        put_basis(index).wait()
        put_residual(index).wait()


def apply(rows, sums, snapshots, chunks):
    snap_rows, cols = snapshots.shape
    count = sums.shape[0]
    width = cols // (2 * chunks)
    dma = pltpu.SemaphoreType.DMA
    anywhere = pl.BlockSpec(memory_space=pl.ANY)
    return pl.pallas_call(
        functools.partial(apply_kernel, chunks, width),
        name="apply",
        out_shape=(jax.ShapeDtypeStruct((count, cols), F32), jax.ShapeDtypeStruct((snap_rows, cols), F32)),
        in_specs=[anywhere, pl.BlockSpec(memory_space=pltpu.VMEM), anywhere],
        out_specs=(anywhere, anywhere),
        scratch_shapes=[
            pltpu.VMEM((2 * chunks, count, width), F32),
            pltpu.VMEM((snap_rows, cols), F32),
            pltpu.VMEM((count, cols), F32),
            pltpu.VMEM((snap_rows, cols), F32),
            pltpu.VMEM((2 * (count + snap_rows), 2 * count), BF16),
            dma((PIECES,)),
            dma,
            dma((SEMS,)),
            dma((SEMS,)),
        ],
        compiler_params=pltpu.CompilerParams(vmem_limit_bytes=48 << 20),
    )(rows, sums, snapshots)


def on_device(snapshots, picks):
    chunks = 32
    rows, sums = gather(snapshots, picks, 48, chunks, 0)
    rows = rows.reshape((2 * chunks,) + rows.shape[2:])
    return apply(rows, sums, snapshots, chunks)


def solution(mesh):
    in_specs = (P("snap", "dof"), P())
    out_specs = (P(None, "dof"), P("snap", "dof"))
    return jax.shard_map(
        on_device, mesh=mesh, in_specs=in_specs, out_specs=out_specs, check_vma=False
    )
```

```python
import functools

import jax
import jax.numpy as jnp
from jax import lax
from jax.experimental import pallas as pl
from jax.experimental.pallas import tpu as pltpu
from jax.sharding import PartitionSpec as P

F32 = jnp.float32
BF16 = jnp.bfloat16
MESH = pl.DeviceIdType.MESH
RING = 4
CORES = 2
PIECES = 4
LAG = 3
TX = 6
SEMS = 16
CHIP_ROWS = 64
CHUNKS = 32
CAPS = (40, 48)
UNROLL = 8


def iota(shape, dim):
    return lax.broadcasted_iota(jnp.int32, shape, dim).astype(F32)


def split(value, parts):
    out = []
    for index in range(parts):
        part = value.astype(BF16)
        out.append(part)
        if index < parts - 1:
            value = value - part.astype(F32)
    return out


def choose(one_hot, rows):
    total = None
    for part in split(rows, 3):
        term = jnp.dot(one_hot, part, preferred_element_type=F32)
        total = term if total is None else total + term
    return total


def plan(picks, cap, x, core):
    steps, block = picks.shape
    count = steps * block
    eye = iota((block, block), 0) == iota((block, block), 1)
    columns = [
        jnp.sum(jnp.where(eye, jnp.broadcast_to(picks[t : t + 1, :], (block, block)), 0.0), axis=1, keepdims=True)
        for t in range(steps)
    ]
    pick = jnp.concatenate(columns, axis=0)
    owner = jnp.floor(pick * (1.0 / CHIP_ROWS))
    row = pick - owner * CHIP_ROWS
    row = jnp.where(row < 32.0, row + 32.0 * core, row - 32.0 * core)
    big_eye = iota((count, count), 0) == iota((count, count), 1)

    def across(column):
        return jnp.sum(jnp.where(big_eye, jnp.broadcast_to(column, (count, count)), 0.0), axis=0, keepdims=True)

    owner_across = across(owner)
    earlier = iota((count, count), 1) < iota((count, count), 0)
    same = jnp.broadcast_to(owner_across, (count, count)) == jnp.broadcast_to(owner, (count, count))
    rank = jnp.sum(jnp.where(same & earlier, 1.0, 0.0), axis=1, keepdims=True)

    before = lax.rem(x + RING - 1, RING).astype(F32)
    here = x.astype(F32)
    after = lax.rem(x + 1, RING).astype(F32)
    across_ring = lax.rem(x + 2, RING).astype(F32)

    def owned(chip):
        return jnp.sum(jnp.where(owner == chip, 1.0, 0.0), axis=0, keepdims=True)

    own_before, own_here, own_after, own_across = owned(before), owned(here), owned(after), owned(across_ring)
    up_before = jnp.clip(cap - own_here, 0.0, own_before)
    up_after = jnp.clip(cap - own_across, 0.0, own_after)
    up_across = jnp.clip(cap - own_before, 0.0, own_across)

    place = jnp.where(owner == here, row, 0.0)
    place = jnp.where(owner == before, 64.0 + rank, place)
    place = jnp.where(owner == after, 64.0 + cap + rank, place)
    far = jnp.where(
        rank < up_across,
        64.0 + 2 * cap + own_before + rank,
        64.0 + 3 * cap + own_after + rank - up_across,
    )
    place = jnp.where(owner == across_ring, far, place)
    width = 64 + 4 * cap
    collect = jnp.where(iota((count, width), 1) == place, 1.0, 0.0).astype(BF16)

    slot = iota((cap, 1), 0)
    rank_across, row_across = across(rank), across(row)
    hit = (jnp.broadcast_to(rank_across, (cap, count)) == iota((cap, count), 0)) & (
        jnp.broadcast_to(owner_across, (cap, count)) == here
    )
    own_row = jnp.sum(jnp.where(hit, jnp.broadcast_to(row_across, (cap, count)), 0.0), axis=1, keepdims=True)
    extra = slot - own_here
    up = jnp.where(extra < up_before, 64.0 + extra, -1.0)
    down = jnp.where(extra < own_after - up_after, 64.0 + cap + up_after + extra, -1.0)
    mine = slot < own_here
    source = jnp.concatenate([jnp.where(mine, own_row, up), jnp.where(mine, own_row, down)], axis=0)
    send = jnp.where(iota((2 * cap, 64 + 2 * cap), 1) == source, 1.0, 0.0).astype(BF16)
    return send, collect


def gather_kernel(
    cap, chunks, width,
    snap_ref, picks_ref, rows_ref, sums_ref,
    picks, local, other, inbox, outbox, rows, send_hot, collect_hot, total, parts, gathered, sums,
    picks_sem, load_sem, swap_send, swap_recv, out_send, in_recv, pass_send, pass_recv, store_sem, sum_send, sum_recv,
):
    half = chunks * width
    snap, dof = lax.axis_index("snap"), lax.axis_index("dof")
    x, core = lax.div(snap, CORES), lax.rem(snap, CORES)
    sibling = (x * CORES + 1 - core, dof)
    up = (lax.rem(x + 1, RING) * CORES + core, dof)
    down = (lax.rem(x + RING - 1, RING) * CORES + core, dof)
    group = RING * RING
    others = [lax.rem(dof + k, group) for k in range(1, group)]
    peers = [sibling, up, down] + [(snap, peer) for peer in others]

    barrier = pltpu.get_barrier_semaphore()
    for peer in peers:
        pl.semaphore_signal(barrier, inc=1, device_id=peer, device_id_type=MESH)

    piece = half // PIECES
    mine = pl.multiple_of(core * half, half)
    theirs = pl.multiple_of((1 - core) * half, half)

    def load(index):
        start = pl.multiple_of(mine + index * piece, piece) if index < PIECES else theirs
        size = piece if index < PIECES else half
        where = (slice(None), pl.ds(start, size))
        return pltpu.make_async_copy(snap_ref.at[where], local.at[where], load_sem.at[index])

    def swap(index):
        start = pl.multiple_of(theirs + index * piece, piece)
        return pltpu.make_async_remote_copy(
            src_ref=snap_ref.at[:, pl.ds(start, piece)],
            dst_ref=other.at[:, pl.ds(index * piece, piece)],
            send_sem=swap_send.at[index],
            recv_sem=swap_recv.at[index],
            device_id=sibling,
            device_id_type=MESH,
        )

    load_picks = pltpu.make_async_copy(picks_ref, picks, picks_sem)
    load_picks.start()
    for index in range(PIECES + 1):
        load(index).start()
    total[...] = jnp.zeros_like(total)
    for way in range(2):
        for slot in range(LAG):
            inbox[way, slot] = jnp.zeros((cap, width), F32)
    pl.semaphore_wait(barrier, len(peers))
    for index in range(PIECES):
        swap(index).start()
    load_picks.wait()
    send, collect = plan(picks[...].astype(F32), cap, x, core)
    send_hot[...] = send
    collect_hot[...] = collect

    def message(step, way):
        return pltpu.make_async_remote_copy(
            src_ref=outbox.at[lax.rem(step, TX), way],
            dst_ref=inbox.at[way, step + LAG],
            send_sem=out_send.at[way, lax.rem(step, TX)],
            recv_sem=in_recv.at[way, lax.rem(step, SEMS)],
            device_id=up if way == 0 else down,
            device_id_type=MESH,
        )

    def hand_over(chunk):
        return pltpu.make_async_remote_copy(
            src_ref=rows.at[core, chunk],
            dst_ref=rows.at[core, chunk],
            send_sem=pass_send.at[lax.rem(chunk, SEMS)],
            recv_sem=pass_recv.at[chunk],
            device_id=sibling,
            device_id_type=MESH,
        )

    def store(which, chunk, sem_row):
        return pltpu.make_async_copy(
            rows.at[which, chunk], rows_ref.at[which, chunk], store_sem.at[sem_row, lax.rem(chunk, SEMS)]
        )

    def local_chunk(base, chunk):
        return local[:, pl.ds(pl.multiple_of(base + chunk * width, width), width)]

    def other_chunk(chunk):
        return other[:, pl.ds(pl.multiple_of(chunk * width, width), width)]

    def add_products(which, picked, snaps):
        picked_parts, snap_parts = split(picked, 2), split(snaps, 2)
        stack = jnp.concatenate([picked_parts[0], snap_parts[0], picked_parts[1], snap_parts[1]], axis=0)
        total[which] += lax.dot_general(stack, stack, (((1,), (1,)), ((), ())), preferred_element_type=F32)

    def body(step, carry):
        for index in range(PIECES):
            @pl.when(step == index * (chunks // PIECES))
            def _():
                load(index).wait()
                swap(index).wait()

        @pl.when(step == LAG)
        def _():
            load(PIECES).wait()

        @pl.when((step >= LAG) & (step < chunks + 2 * LAG))
        def _():
            for way in range(2):
                message(step - LAG, way).wait_recv()

        @pl.when(step < chunks + LAG)
        def _():
            @pl.when(step >= TX)
            def _():
                for way in range(2):
                    message(step - TX, way).wait_send()

            chunk = jnp.minimum(step, chunks - 1)
            stage = jnp.concatenate(
                [local_chunk(mine, chunk), other_chunk(chunk), inbox[0, step], inbox[1, step]], axis=0
            )
            sent = choose(send_hot[...], stage)
            slot = lax.rem(step, TX)
            outbox[slot, 0] = sent[:cap]
            outbox[slot, 1] = sent[cap:]
            for way in range(2):
                message(step, way).start()

        @pl.when((step >= 2 * LAG) & (step < chunks + 2 * LAG))
        def _():
            chunk = step - 2 * LAG
            here = local_chunk(mine, chunk)
            stage = jnp.concatenate(
                [here, other_chunk(chunk), inbox[0, step - LAG], inbox[1, step - LAG], inbox[0, step], inbox[1, step]],
                axis=0,
            )
            picked = choose(collect_hot[...], stage)
            rows[core, chunk] = picked

            @pl.when(chunk >= SEMS)
            def _():
                hand_over(chunk - SEMS).wait_send()
                store(core, chunk - SEMS, 0).wait()

            hand_over(chunk).start()
            store(core, chunk, 0).start()
            add_products(core, picked, here)

        @pl.when(step >= 2 * LAG + 1)
        def _():
            chunk = step - 2 * LAG - 1
            hand_over(chunk).wait_recv()

            @pl.when(chunk >= SEMS)
            def _():
                store(1 - core, chunk - SEMS, 1).wait()

            store(1 - core, chunk, 1).start()
            add_products(1 - core, rows[1 - core, chunk], local_chunk(theirs, chunk))

        return carry

    lax.fori_loop(0, chunks + 2 * LAG + 1, body, 0)

    both = total[0] + total[1]
    wide = both.shape[0] // 2
    both = (both[:wide, :wide] + both[wide:, wide:]) + (both[:wide, wide:] + both[wide:, :wide])
    share = wide // group
    for index in range(group):
        parts[index] = both[index * share : (index + 1) * share]

    def give(k):
        return pltpu.make_async_remote_copy(
            src_ref=parts.at[others[k]],
            dst_ref=gathered.at[dof],
            send_sem=sum_send.at[0, k],
            recv_sem=sum_recv.at[0, k],
            device_id=(snap, others[k]),
            device_id_type=MESH,
        )

    def tell(k):
        return pltpu.make_async_remote_copy(
            src_ref=sums.at[dof],
            dst_ref=sums.at[dof],
            send_sem=sum_send.at[1, k],
            recv_sem=sum_recv.at[1, k],
            device_id=(snap, others[k]),
            device_id_type=MESH,
        )

    for k in range(group - 1):
        give(k).start()
    gathered[dof] = parts[dof]
    for k in range(group - 1):
        give(k).wait_recv()
    terms = [gathered[index] for index in range(group)]
    while len(terms) > 1:
        terms = [terms[i] + terms[i + 1] for i in range(0, len(terms), 2)]
    sums[dof] = terms[0] * (1.0 / (2 * half * group))
    for k in range(group - 1):
        tell(k).start()
    for k in range(group - 1):
        give(k).wait_send()
    for k in range(group - 1):
        tell(k).wait()
    for index in range(sums_ref.shape[0] // share):
        sums_ref[index * share : (index + 1) * share, :] = sums[index]

    for step in range(chunks + LAG - TX, chunks + LAG):
        for way in range(2):
            message(step, way).wait_send()
    for chunk in range(chunks - SEMS, chunks):
        hand_over(chunk).wait_send()
        store(core, chunk, 0).wait()
        store(1 - core, chunk, 1).wait()


def gather(snapshots, picks, cap, chunks, collective_id):
    snap_rows, cols = snapshots.shape
    steps, block = picks.shape
    snapshots = pltpu.with_memory_space_constraint(snapshots, pltpu.HBM)
    picks = pltpu.with_memory_space_constraint(picks, pltpu.HBM)
    count = steps * block
    half = cols // 2
    width = half // chunks
    wide = count + snap_rows
    group = RING * RING
    dma = pltpu.SemaphoreType.DMA
    return pl.pallas_call(
        functools.partial(gather_kernel, cap, chunks, width),
        name=f"gather_{cap}",
        out_shape=(
            jax.ShapeDtypeStruct((2, chunks, count, width), F32),
            jax.ShapeDtypeStruct((count, count + snap_rows), F32),
        ),
        in_specs=[pl.BlockSpec(memory_space=pl.ANY), pl.BlockSpec(memory_space=pl.ANY)],
        out_specs=(pl.BlockSpec(memory_space=pl.ANY), pl.BlockSpec(memory_space=pltpu.VMEM)),
        scratch_shapes=[
            pltpu.VMEM((steps, block), jnp.int32),
            pltpu.VMEM((snap_rows, cols), F32),
            pltpu.VMEM((snap_rows, half), F32),
            pltpu.VMEM((2, chunks + 2 * LAG, cap, width), F32),
            pltpu.VMEM((TX, 2, cap, width), F32),
            pltpu.VMEM((2, chunks, count, width), F32),
            pltpu.VMEM((2 * cap, 64 + 2 * cap), BF16),
            pltpu.VMEM((count, 64 + 4 * cap), BF16),
            pltpu.VMEM((2, 2 * wide, 2 * wide), F32),
            pltpu.VMEM((group, wide // group, wide), F32),
            pltpu.VMEM((group, wide // group, wide), F32),
            pltpu.VMEM((group, wide // group, wide), F32),
            dma,
            dma((PIECES + 1,)),
            dma((PIECES,)),
            dma((PIECES,)),
            dma((2, TX)),
            dma((2, SEMS)),
            dma((SEMS,)),
            dma((chunks,)),
            dma((2, SEMS)),
            dma((2, group - 1)),
            dma((2, group - 1)),
        ],
        compiler_params=pltpu.CompilerParams(
            collective_id=collective_id, has_side_effects=True, vmem_limit_bytes=48 << 20
        ),
    )(snapshots, picks)


def eliminate(sums, count):
    tiles = count // 8
    lanes = sums.shape[1]
    shape = (8, lanes)
    left = [sums[8 * t : 8 * t + 8, :] for t in range(tiles)]
    right = [jnp.where(iota(shape, 1) == iota(shape, 0) + 8.0 * t, 1.0, 0.0) for t in range(tiles)]
    sub = iota(shape, 0)
    pivots = []

    def spread_row(tile, k):
        return jnp.broadcast_to(tile[k : k + 1, :], shape)

    def stack(values):
        out = values[0]
        for k in range(1, 8):
            out = jnp.where(sub == k, values[k], out)
        return out

    for b in range(tiles):
        columns = {
            t: [jnp.broadcast_to(left[t][:, 8 * b + k : 8 * b + k + 1], shape) for k in range(8)]
            for t in range(b, tiles)
        }
        left_rows = [spread_row(left[b], k) for k in range(8)]
        right_rows = [spread_row(right[b], k) for k in range(8)]
        corner = [[spread_row(columns[b][k], i) for k in range(i + 1)] for i in range(8)]
        inverse = []
        for k in range(8):
            inverse.append(1.0 / corner[k][k])
            factor = [None] * (k + 1) + [corner[i][k] * inverse[k] for i in range(k + 1, 8)]
            for i in range(k + 1, 8):
                for j in range(k + 1, i + 1):
                    corner[i][j] = corner[i][j] - factor[i] * corner[j][k]
            for i in range(k + 1, 8):
                left_rows[i] = left_rows[i] - factor[i] * left_rows[k]
                right_rows[i] = right_rows[i] - factor[i] * right_rows[k]
        left[b] = stack(left_rows)
        right[b] = stack(right_rows)
        pivots.append(stack([corner[k][k] for k in range(8)]))
        for t in range(b + 1, tiles):
            for k in range(8):
                factor = columns[t][k] * inverse[k]
                for later in range(k + 1, 8):
                    columns[t][later] = columns[t][later] - factor * corner[later][k]
                left[t] = left[t] - factor * left_rows[k]
                right[t] = right[t] - factor * right_rows[k]
    return jnp.concatenate(left, axis=0), jnp.concatenate(right, axis=0), jnp.concatenate(pivots, axis=0)


def apply_kernel(
    chunks, width, rows_ref, sums_ref, snap_ref, basis_ref, residual_ref,
    rows, snaps, basis, residual, weights, rows_sem, snap_sem, basis_sem, residual_sem,
):
    count = basis.shape[0]
    group = 2 * chunks // PIECES

    def load_rows(index):
        where = pl.ds(index * group, group)
        return pltpu.make_async_copy(rows_ref.at[where], rows.at[where], rows_sem.at[index])

    for index in range(PIECES):
        load_rows(index).start()
    load_snaps = pltpu.make_async_copy(snap_ref, snaps, snap_sem)
    load_snaps.start()

    left, right, pivots = eliminate(sums_ref[...], count)
    inverse = right[:, :count]
    cross = left[:, count:]
    scale = lax.rsqrt(pivots[:, :1])
    to_basis = inverse * scale
    coefficients = cross * (1.0 / pivots[:, : cross.shape[1]])
    to_residual = lax.dot_general(
        coefficients, inverse, (((0,), (0,)), ((), ())),
        precision=lax.Precision.HIGHEST, preferred_element_type=F32,
    )
    high, low = split(jnp.concatenate([to_basis, to_residual], axis=0), 2)
    weights[...] = jnp.concatenate([high, high, low], axis=1)

    def columns(index):
        return (slice(None), pl.ds(pl.multiple_of(index * width, width), width))

    def put(source, target, sem, index):
        wide = (slice(None), pl.ds(pl.multiple_of(index * (UNROLL * width), UNROLL * width), UNROLL * width))
        return pltpu.make_async_copy(source.at[wide], target.at[wide], sem.at[lax.rem(index, SEMS)])

    def put_basis(index):
        return put(basis, basis_ref, basis_sem, index)

    def put_residual(index):
        return put(residual, residual_ref, residual_sem, index)

    load_snaps.wait()
    steps = 2 * chunks // UNROLL

    def body(step, carry):
        for piece in range(PIECES):
            @pl.when(step * UNROLL == piece * group)
            def _():
                load_rows(piece).wait()

        for k in range(UNROLL):
            index = step * UNROLL + k
            high, low = split(rows[index], 2)
            stack = jnp.concatenate([high, low, high], axis=0)
            out = jnp.dot(weights[...], stack, preferred_element_type=F32)
            where = columns(index)
            basis[where] = out[:count]
            residual[where] = snaps[where] - out[count:]

        put_basis(step).start()
        put_residual(step).start()
        return carry

    lax.fori_loop(0, steps, body, 0)
    for step in range(steps):
        put_basis(step).wait()
        put_residual(step).wait()


def apply(rows, sums, snapshots, chunks):
    snap_rows, cols = snapshots.shape
    snapshots = pltpu.with_memory_space_constraint(snapshots, pltpu.HBM)
    count = sums.shape[0]
    width = cols // (2 * chunks)
    dma = pltpu.SemaphoreType.DMA
    anywhere = pl.BlockSpec(memory_space=pl.ANY)
    return pl.pallas_call(
        functools.partial(apply_kernel, chunks, width),
        name="apply",
        out_shape=(jax.ShapeDtypeStruct((count, cols), F32), jax.ShapeDtypeStruct((snap_rows, cols), F32)),
        in_specs=[anywhere, pl.BlockSpec(memory_space=pltpu.VMEM), anywhere],
        out_specs=(anywhere, anywhere),
        scratch_shapes=[
            pltpu.VMEM((2 * chunks, count, width), F32),
            pltpu.VMEM((snap_rows, cols), F32),
            pltpu.VMEM((count, cols), F32),
            pltpu.VMEM((snap_rows, cols), F32),
            pltpu.VMEM((count + snap_rows, 3 * count), BF16),
            dma((PIECES,)),
            dma,
            dma((SEMS,)),
            dma((SEMS,)),
        ],
        compiler_params=pltpu.CompilerParams(vmem_limit_bytes=48 << 20),
    )(rows, sums, snapshots)


def on_device(snapshots, picks):
    chunks = CHUNKS
    chips = picks // CHIP_ROWS
    owned = [jnp.sum((chips == chip).astype(jnp.int32)) for chip in range(RING)]
    most = functools.reduce(jnp.maximum, owned)
    least = functools.reduce(jnp.minimum, owned)
    small = (most <= CAPS[0]) & (picks.size - least <= 2 * CAPS[0])
    rows, sums = lax.cond(
        small,
        lambda s, p: gather(s, p, CAPS[0], chunks, 0),
        lambda s, p: gather(s, p, CAPS[1], chunks, 1),
        snapshots,
        picks,
    )
    rows = rows.reshape((2 * chunks,) + rows.shape[2:])
    return apply(rows, sums, snapshots, chunks)


def solution(mesh):
    in_specs = (P("snap", "dof"), P())
    out_specs = (P(None, "dof"), P("snap", "dof"))
    return jax.shard_map(
        on_device, mesh=mesh, in_specs=in_specs, out_specs=out_specs, check_vma=False
    )
```

```python
import functools

import jax
import jax.numpy as jnp
from jax import lax
from jax.experimental import pallas as pl
from jax.experimental.pallas import tpu as pltpu
from jax.sharding import PartitionSpec as P

F32 = jnp.float32
BF16 = jnp.bfloat16
MESH = pl.DeviceIdType.MESH
RING = 4
CORES = 2
PIECES = 4
LAG = 3
TX = 6
SEMS = 16
CHIP_ROWS = 64
CHUNKS = 32
SMALL = (40, 32, 24)
LARGE = (48, 48, 48)
UNROLL = 8


def iota(shape, dim):
    return lax.broadcasted_iota(jnp.int32, shape, dim).astype(F32)


def split(value, parts):
    out = []
    for index in range(parts):
        part = value.astype(BF16)
        out.append(part)
        if index < parts - 1:
            value = value - part.astype(F32)
    return out


def choose(one_hot, rows):
    total = None
    for part in split(rows, 3):
        term = jnp.dot(one_hot, part, preferred_element_type=F32)
        total = term if total is None else total + term
    return total


def plan(picks, cap, x, core):
    steps, block = picks.shape
    count = steps * block
    eye = iota((block, block), 0) == iota((block, block), 1)
    columns = [
        jnp.sum(jnp.where(eye, jnp.broadcast_to(picks[t : t + 1, :], (block, block)), 0.0), axis=1, keepdims=True)
        for t in range(steps)
    ]
    pick = jnp.concatenate(columns, axis=0)
    owner = jnp.floor(pick * (1.0 / CHIP_ROWS))
    row = pick - owner * CHIP_ROWS
    row = jnp.where(row < 32.0, row + 32.0 * core, row - 32.0 * core)
    big_eye = iota((count, count), 0) == iota((count, count), 1)

    def across(column):
        return jnp.sum(jnp.where(big_eye, jnp.broadcast_to(column, (count, count)), 0.0), axis=0, keepdims=True)

    owner_across = across(owner)
    earlier = iota((count, count), 1) < iota((count, count), 0)
    same = jnp.broadcast_to(owner_across, (count, count)) == jnp.broadcast_to(owner, (count, count))
    rank = jnp.sum(jnp.where(same & earlier, 1.0, 0.0), axis=1, keepdims=True)

    before = lax.rem(x + RING - 1, RING).astype(F32)
    here = x.astype(F32)
    after = lax.rem(x + 1, RING).astype(F32)
    across_ring = lax.rem(x + 2, RING).astype(F32)

    def owned(chip):
        return jnp.sum(jnp.where(owner == chip, 1.0, 0.0), axis=0, keepdims=True)

    own_before, own_here, own_after, own_across = owned(before), owned(here), owned(after), owned(across_ring)

    def upward(own, own_down, own_up):
        return jnp.minimum(jnp.maximum(jnp.floor(own * 0.5), own + own_down - cap), cap - own_up)

    up_before = upward(own_before, own_across, own_here)
    up_after = upward(own_after, own_here, own_across)
    up_across = upward(own_across, own_after, own_before)

    place = jnp.where(owner == here, row, 0.0)
    place = jnp.where(owner == before, 64.0 + rank, place)
    place = jnp.where(owner == after, 64.0 + cap + rank, place)
    width = 64 + 4 * cap

    def collect(skip_before, skip_after):
        far = jnp.where(
            rank < up_across,
            64.0 + 2 * cap + skip_before + rank,
            64.0 + 3 * cap + skip_after + rank - up_across,
        )
        source = jnp.where(owner == across_ring, far, place)
        return jnp.where(iota((count, width), 1) == source, 1.0, 0.0).astype(BF16)

    slot = iota((cap, 1), 0)
    rank_across, row_across = across(rank), across(row)
    hit = (jnp.broadcast_to(rank_across, (cap, count)) == iota((cap, count), 0)) & (
        jnp.broadcast_to(owner_across, (cap, count)) == here
    )
    own_row = jnp.sum(jnp.where(hit, jnp.broadcast_to(row_across, (cap, count)), 0.0), axis=1, keepdims=True)

    def forward(extra):
        return (
            jnp.where(extra < up_before, 64.0 + extra, -1.0),
            jnp.where(extra < own_after - up_after, 64.0 + cap + up_after + extra, -1.0),
        )

    def send(columns):
        source = jnp.concatenate(columns, axis=0)
        return jnp.where(iota((2 * cap, 64 + 2 * cap), 1) == source, 1.0, 0.0).astype(BF16)

    mixed = [jnp.where(slot < own_here, own_row, way) for way in forward(slot - own_here)]
    return (send(mixed), send(forward(slot))), (collect(own_before, own_after), collect(0.0, 0.0))


def gather_kernel(
    slots, chunks, width,
    snap_ref, picks_ref, rows_ref, sums_ref,
    picks, local, other, inbox, outbox, rows, send_hot, collect_hot, total, parts, gathered, sums,
    picks_sem, load_sem, swap_send, swap_recv, out_send, in_recv, pass_send, pass_recv, store_sem, sum_send, sum_recv,
):
    cap, head, tail = slots
    half = chunks * width
    snap, dof = lax.axis_index("snap"), lax.axis_index("dof")
    x, core = lax.div(snap, CORES), lax.rem(snap, CORES)
    sibling = (x * CORES + 1 - core, dof)
    up = (lax.rem(x + 1, RING) * CORES + core, dof)
    down = (lax.rem(x + RING - 1, RING) * CORES + core, dof)
    group = RING * RING
    others = [lax.rem(dof + k, group) for k in range(1, group)]
    peers = [sibling, up, down] + [(snap, peer) for peer in others]

    barrier = pltpu.get_barrier_semaphore()
    for peer in peers:
        pl.semaphore_signal(barrier, inc=1, device_id=peer, device_id_type=MESH)

    piece = half // PIECES
    mine = pl.multiple_of(core * half, half)
    theirs = pl.multiple_of((1 - core) * half, half)

    def load(index):
        start = pl.multiple_of(mine + index * piece, piece) if index < PIECES else theirs
        size = piece if index < PIECES else half
        where = (slice(None), pl.ds(start, size))
        return pltpu.make_async_copy(snap_ref.at[where], local.at[where], load_sem.at[index])

    def swap(index):
        start = pl.multiple_of(theirs + index * piece, piece)
        return pltpu.make_async_remote_copy(
            src_ref=snap_ref.at[:, pl.ds(start, piece)],
            dst_ref=other.at[:, pl.ds(index * piece, piece)],
            send_sem=swap_send.at[index],
            recv_sem=swap_recv.at[index],
            device_id=sibling,
            device_id_type=MESH,
        )

    load_picks = pltpu.make_async_copy(picks_ref, picks, picks_sem)
    load_picks.start()
    for index in range(PIECES + 1):
        load(index).start()
    total[...] = jnp.zeros_like(total)
    for way in range(2):
        for slot in range(LAG):
            inbox[way, slot] = jnp.zeros((cap, width), F32)
            if head < cap:
                inbox[way, LAG + slot, head:, :] = jnp.zeros((cap - head, width), F32)
            if tail < cap:
                inbox[way, LAG + chunks + slot, tail:, :] = jnp.zeros((cap - tail, width), F32)
    pl.semaphore_wait(barrier, len(peers))
    for index in range(PIECES):
        swap(index).start()
    load_picks.wait()
    send, collect = plan(picks[...].astype(F32), cap, x, core)
    for late in range(2):
        send_hot[late] = send[late]
        collect_hot[late] = collect[late]

    def message(step, way, size):
        return pltpu.make_async_remote_copy(
            src_ref=outbox.at[lax.rem(step, TX), way, pl.ds(0, size)],
            dst_ref=inbox.at[way, step + LAG, pl.ds(0, size)],
            send_sem=out_send.at[way, lax.rem(step, TX)],
            recv_sem=in_recv.at[way, lax.rem(step, SEMS)],
            device_id=up if way == 0 else down,
            device_id_type=MESH,
        )

    def messages(step, act):
        if head == cap and tail == cap:
            for way in range(2):
                act(message(step, way, cap))
            return
        for size, when in (
            (head, step < LAG),
            (cap, (step >= LAG) & (step < chunks)),
            (tail, step >= chunks),
        ):
            @pl.when(when)
            def _():
                for way in range(2):
                    act(message(step, way, size))

    def hand_over(chunk):
        return pltpu.make_async_remote_copy(
            src_ref=rows.at[core, chunk],
            dst_ref=rows.at[core, chunk],
            send_sem=pass_send.at[lax.rem(chunk, SEMS)],
            recv_sem=pass_recv.at[chunk],
            device_id=sibling,
            device_id_type=MESH,
        )

    def store(which, chunk, sem_row):
        return pltpu.make_async_copy(
            rows.at[which, chunk], rows_ref.at[which, chunk], store_sem.at[sem_row, lax.rem(chunk, SEMS)]
        )

    def local_chunk(base, chunk):
        return local[:, pl.ds(pl.multiple_of(base + chunk * width, width), width)]

    def other_chunk(chunk):
        return other[:, pl.ds(pl.multiple_of(chunk * width, width), width)]

    def add_products(which, picked, snaps):
        picked_parts, snap_parts = split(picked, 2), split(snaps, 2)
        stack = jnp.concatenate([picked_parts[0], snap_parts[0], picked_parts[1], snap_parts[1]], axis=0)
        total[which] += lax.dot_general(stack, stack, (((1,), (1,)), ((), ())), preferred_element_type=F32)

    def body(step, carry):
        for index in range(PIECES):
            @pl.when(step == index * (chunks // PIECES))
            def _():
                load(index).wait()
                swap(index).wait()

        @pl.when(step == LAG)
        def _():
            load(PIECES).wait()

        @pl.when((step >= LAG) & (step < chunks + 2 * LAG))
        def _():
            messages(step - LAG, lambda copy: copy.wait_recv())

        @pl.when(step < chunks + LAG)
        def _():
            @pl.when(step >= TX)
            def _():
                messages(step - TX, lambda copy: copy.wait_send())

            chunk = jnp.minimum(step, chunks - 1)
            stage = jnp.concatenate(
                [local_chunk(mine, chunk), other_chunk(chunk), inbox[0, step], inbox[1, step]], axis=0
            )
            sent = choose(send_hot[jnp.where(step < chunks, 0, 1)], stage)
            slot = lax.rem(step, TX)
            outbox[slot, 0] = sent[:cap]
            outbox[slot, 1] = sent[cap:]
            messages(step, lambda copy: copy.start())

        @pl.when((step >= 2 * LAG) & (step < chunks + 2 * LAG))
        def _():
            chunk = step - 2 * LAG
            here = local_chunk(mine, chunk)
            stage = jnp.concatenate(
                [here, other_chunk(chunk), inbox[0, step - LAG], inbox[1, step - LAG], inbox[0, step], inbox[1, step]],
                axis=0,
            )
            picked = choose(collect_hot[jnp.where(chunk < chunks - LAG, 0, 1)], stage)
            rows[core, chunk] = picked

            @pl.when(chunk >= SEMS)
            def _():
                hand_over(chunk - SEMS).wait_send()
                store(core, chunk - SEMS, 0).wait()

            hand_over(chunk).start()
            store(core, chunk, 0).start()
            add_products(core, picked, here)

        @pl.when(step >= 2 * LAG + 1)
        def _():
            chunk = step - 2 * LAG - 1
            hand_over(chunk).wait_recv()

            @pl.when(chunk >= SEMS)
            def _():
                store(1 - core, chunk - SEMS, 1).wait()

            store(1 - core, chunk, 1).start()
            add_products(1 - core, rows[1 - core, chunk], local_chunk(theirs, chunk))

        return carry

    lax.fori_loop(0, chunks + 2 * LAG + 1, body, 0)

    both = total[0] + total[1]
    wide = both.shape[0] // 2
    both = (both[:wide, :wide] + both[wide:, wide:]) + (both[:wide, wide:] + both[wide:, :wide])
    share = wide // group
    for index in range(group):
        parts[index] = both[index * share : (index + 1) * share]

    def give(k):
        return pltpu.make_async_remote_copy(
            src_ref=parts.at[others[k]],
            dst_ref=gathered.at[dof],
            send_sem=sum_send.at[0, k],
            recv_sem=sum_recv.at[0, k],
            device_id=(snap, others[k]),
            device_id_type=MESH,
        )

    def tell(k):
        return pltpu.make_async_remote_copy(
            src_ref=sums.at[dof],
            dst_ref=sums.at[dof],
            send_sem=sum_send.at[1, k],
            recv_sem=sum_recv.at[1, k],
            device_id=(snap, others[k]),
            device_id_type=MESH,
        )

    for k in range(group - 1):
        give(k).start()
    gathered[dof] = parts[dof]
    for k in range(group - 1):
        give(k).wait_recv()
    terms = [gathered[index] for index in range(group)]
    while len(terms) > 1:
        terms = [terms[i] + terms[i + 1] for i in range(0, len(terms), 2)]
    sums[dof] = terms[0] * (1.0 / (2 * half * group))
    for k in range(group - 1):
        tell(k).start()
    for k in range(group - 1):
        give(k).wait_send()
    for k in range(group - 1):
        tell(k).wait()
    for index in range(sums_ref.shape[0] // share):
        sums_ref[index * share : (index + 1) * share, :] = sums[index]

    for step in range(chunks + LAG - TX, chunks + LAG):
        for way in range(2):
            message(step, way, cap if step < chunks else tail).wait_send()
    for chunk in range(chunks - SEMS, chunks):
        hand_over(chunk).wait_send()
        store(core, chunk, 0).wait()
        store(1 - core, chunk, 1).wait()


def gather(snapshots, picks, slots, chunks, collective_id):
    cap = slots[0]
    snap_rows, cols = snapshots.shape
    steps, block = picks.shape
    snapshots = pltpu.with_memory_space_constraint(snapshots, pltpu.HBM)
    picks = pltpu.with_memory_space_constraint(picks, pltpu.HBM)
    count = steps * block
    half = cols // 2
    width = half // chunks
    wide = count + snap_rows
    group = RING * RING
    dma = pltpu.SemaphoreType.DMA
    return pl.pallas_call(
        functools.partial(gather_kernel, slots, chunks, width),
        name=f"gather_{cap}",
        out_shape=(
            jax.ShapeDtypeStruct((2, chunks, count, width), F32),
            jax.ShapeDtypeStruct((count, count + snap_rows), F32),
        ),
        in_specs=[pl.BlockSpec(memory_space=pl.ANY), pl.BlockSpec(memory_space=pl.ANY)],
        out_specs=(pl.BlockSpec(memory_space=pl.ANY), pl.BlockSpec(memory_space=pltpu.VMEM)),
        scratch_shapes=[
            pltpu.VMEM((steps, block), jnp.int32),
            pltpu.VMEM((snap_rows, cols), F32),
            pltpu.VMEM((snap_rows, half), F32),
            pltpu.VMEM((2, chunks + 2 * LAG, cap, width), F32),
            pltpu.VMEM((TX, 2, cap, width), F32),
            pltpu.VMEM((2, chunks, count, width), F32),
            pltpu.VMEM((2, 2 * cap, 64 + 2 * cap), BF16),
            pltpu.VMEM((2, count, 64 + 4 * cap), BF16),
            pltpu.VMEM((2, 2 * wide, 2 * wide), F32),
            pltpu.VMEM((group, wide // group, wide), F32),
            pltpu.VMEM((group, wide // group, wide), F32),
            pltpu.VMEM((group, wide // group, wide), F32),
            dma,
            dma((PIECES + 1,)),
            dma((PIECES,)),
            dma((PIECES,)),
            dma((2, TX)),
            dma((2, SEMS)),
            dma((SEMS,)),
            dma((chunks,)),
            dma((2, SEMS)),
            dma((2, group - 1)),
            dma((2, group - 1)),
        ],
        compiler_params=pltpu.CompilerParams(
            collective_id=collective_id, has_side_effects=True, vmem_limit_bytes=48 << 20
        ),
    )(snapshots, picks)


def eliminate(sums, count):
    tiles = count // 8
    lanes = sums.shape[1]
    shape = (8, lanes)
    left = [sums[8 * t : 8 * t + 8, :] for t in range(tiles)]
    right = [jnp.where(iota(shape, 1) == iota(shape, 0) + 8.0 * t, 1.0, 0.0) for t in range(tiles)]
    sub = iota(shape, 0)
    pivots = []

    def spread_row(tile, k):
        return jnp.broadcast_to(tile[k : k + 1, :], shape)

    def stack(values):
        out = values[0]
        for k in range(1, 8):
            out = jnp.where(sub == k, values[k], out)
        return out

    for b in range(tiles):
        columns = {
            t: [jnp.broadcast_to(left[t][:, 8 * b + k : 8 * b + k + 1], shape) for k in range(8)]
            for t in range(b, tiles)
        }
        left_rows = [spread_row(left[b], k) for k in range(8)]
        right_rows = [spread_row(right[b], k) for k in range(8)]
        corner = [[spread_row(columns[b][k], i) for k in range(i + 1)] for i in range(8)]
        inverse = []
        for k in range(8):
            inverse.append(1.0 / corner[k][k])
            factor = [None] * (k + 1) + [corner[i][k] * inverse[k] for i in range(k + 1, 8)]
            for i in range(k + 1, 8):
                for j in range(k + 1, i + 1):
                    corner[i][j] = corner[i][j] - factor[i] * corner[j][k]
            for i in range(k + 1, 8):
                left_rows[i] = left_rows[i] - factor[i] * left_rows[k]
                right_rows[i] = right_rows[i] - factor[i] * right_rows[k]
        left[b] = stack(left_rows)
        right[b] = stack(right_rows)
        pivots.append(stack([corner[k][k] for k in range(8)]))
        for t in range(b + 1, tiles):
            for k in range(8):
                factor = columns[t][k] * inverse[k]
                for later in range(k + 1, 8):
                    columns[t][later] = columns[t][later] - factor * corner[later][k]
                left[t] = left[t] - factor * left_rows[k]
                right[t] = right[t] - factor * right_rows[k]
    return jnp.concatenate(left, axis=0), jnp.concatenate(right, axis=0), jnp.concatenate(pivots, axis=0)


def apply_kernel(
    chunks, width, rows_ref, sums_ref, snap_ref, basis_ref, residual_ref,
    rows, snaps, basis, residual, weights, rows_sem, snap_sem, basis_sem, residual_sem,
):
    count = basis.shape[0]
    group = 2 * chunks // PIECES

    def load_rows(index):
        where = pl.ds(index * group, group)
        return pltpu.make_async_copy(rows_ref.at[where], rows.at[where], rows_sem.at[index])

    for index in range(PIECES):
        load_rows(index).start()
    load_snaps = pltpu.make_async_copy(snap_ref, snaps, snap_sem)
    load_snaps.start()

    left, right, pivots = eliminate(sums_ref[...], count)
    inverse = right[:, :count]
    cross = left[:, count:]
    scale = lax.rsqrt(pivots[:, :1])
    to_basis = inverse * scale
    coefficients = cross * (1.0 / pivots[:, : cross.shape[1]])
    to_residual = lax.dot_general(
        coefficients, inverse, (((0,), (0,)), ((), ())),
        precision=lax.Precision.HIGHEST, preferred_element_type=F32,
    )
    high, low = split(jnp.concatenate([to_basis, to_residual], axis=0), 2)
    weights[...] = jnp.concatenate([high, high, low], axis=1)

    def columns(index):
        return (slice(None), pl.ds(pl.multiple_of(index * width, width), width))

    def put(source, target, sem, index):
        wide = (slice(None), pl.ds(pl.multiple_of(index * (UNROLL * width), UNROLL * width), UNROLL * width))
        return pltpu.make_async_copy(source.at[wide], target.at[wide], sem.at[lax.rem(index, SEMS)])

    def put_basis(index):
        return put(basis, basis_ref, basis_sem, index)

    def put_residual(index):
        return put(residual, residual_ref, residual_sem, index)

    load_snaps.wait()
    steps = 2 * chunks // UNROLL

    def body(step, carry):
        for piece in range(PIECES):
            @pl.when(step * UNROLL == piece * group)
            def _():
                load_rows(piece).wait()

        for k in range(UNROLL):
            index = step * UNROLL + k
            high, low = split(rows[index], 2)
            stack = jnp.concatenate([high, low, high], axis=0)
            out = jnp.dot(weights[...], stack, preferred_element_type=F32)
            where = columns(index)
            basis[where] = out[:count]
            residual[where] = snaps[where] - out[count:]

        put_basis(step).start()
        put_residual(step).start()
        return carry

    lax.fori_loop(0, steps, body, 0)
    for step in range(steps):
        put_basis(step).wait()
        put_residual(step).wait()


def apply(rows, sums, snapshots, chunks):
    snap_rows, cols = snapshots.shape
    snapshots = pltpu.with_memory_space_constraint(snapshots, pltpu.HBM)
    count = sums.shape[0]
    width = cols // (2 * chunks)
    dma = pltpu.SemaphoreType.DMA
    anywhere = pl.BlockSpec(memory_space=pl.ANY)
    return pl.pallas_call(
        functools.partial(apply_kernel, chunks, width),
        name="apply",
        out_shape=(jax.ShapeDtypeStruct((count, cols), F32), jax.ShapeDtypeStruct((snap_rows, cols), F32)),
        in_specs=[anywhere, pl.BlockSpec(memory_space=pltpu.VMEM), anywhere],
        out_specs=(anywhere, anywhere),
        scratch_shapes=[
            pltpu.VMEM((2 * chunks, count, width), F32),
            pltpu.VMEM((snap_rows, cols), F32),
            pltpu.VMEM((count, cols), F32),
            pltpu.VMEM((snap_rows, cols), F32),
            pltpu.VMEM((count + snap_rows, 3 * count), BF16),
            dma((PIECES,)),
            dma,
            dma((SEMS,)),
            dma((SEMS,)),
        ],
        compiler_params=pltpu.CompilerParams(vmem_limit_bytes=48 << 20),
    )(rows, sums, snapshots)


def on_device(snapshots, picks):
    chunks = CHUNKS
    counts = jnp.sum(1 << (8 * (picks // CHIP_ROWS)))
    owned = [(counts >> (8 * chip)) & 255 for chip in range(RING)]
    most = functools.reduce(jnp.maximum, owned)
    least = functools.reduce(jnp.minimum, owned)
    cap, head, _ = SMALL
    small = (most <= head) & (picks.size - least <= 2 * cap)
    rows, sums = lax.cond(
        small,
        lambda s, p: gather(s, p, SMALL, chunks, 0),
        lambda s, p: gather(s, p, LARGE, chunks, 1),
        snapshots,
        picks,
    )
    rows = rows.reshape((2 * chunks,) + rows.shape[2:])
    return apply(rows, sums, snapshots, chunks)


def solution(mesh):
    in_specs = (P("snap", "dof"), P())
    out_specs = (P(None, "dof"), P("snap", "dof"))
    return jax.shard_map(
        on_device, mesh=mesh, in_specs=in_specs, out_specs=out_specs, check_vma=False
    )
```

```python
import functools

import jax
import jax.numpy as jnp
from jax import lax
from jax.experimental import pallas as pl
from jax.experimental.pallas import tpu as pltpu
from jax.sharding import PartitionSpec as P

F32 = jnp.float32
BF16 = jnp.bfloat16
MESH = pl.DeviceIdType.MESH
RING = 4
CORES = 2
PIECES = 4
LAG = 3
TX = 6
SEMS = 16
CHIP_ROWS = 64
CHUNKS = 32
SMALL = (40, 32, 24)
LARGE = (48, 48, 48)
UNROLL = 8


def iota(shape, dim):
    return lax.broadcasted_iota(jnp.int32, shape, dim).astype(F32)


def split(value, parts):
    out = []
    for index in range(parts):
        part = value.astype(BF16)
        out.append(part)
        if index < parts - 1:
            value = value - part.astype(F32)
    return out


def choose(one_hot, rows):
    total = None
    for part in split(rows, 3):
        term = jnp.dot(one_hot, part, preferred_element_type=F32)
        total = term if total is None else total + term
    return total


def plan(picks, cap, x, core):
    steps, block = picks.shape
    count = steps * block
    eye = iota((block, block), 0) == iota((block, block), 1)
    columns = [
        jnp.sum(jnp.where(eye, jnp.broadcast_to(picks[t : t + 1, :], (block, block)), 0.0), axis=1, keepdims=True)
        for t in range(steps)
    ]
    pick = jnp.concatenate(columns, axis=0)
    owner = jnp.floor(pick * (1.0 / CHIP_ROWS))
    row = pick - owner * CHIP_ROWS
    row = jnp.where(row < 32.0, row + 32.0 * core, row - 32.0 * core)
    big_eye = iota((count, count), 0) == iota((count, count), 1)

    def across(column):
        return jnp.sum(jnp.where(big_eye, jnp.broadcast_to(column, (count, count)), 0.0), axis=0, keepdims=True)

    owner_across = across(owner)
    earlier = iota((count, count), 1) < iota((count, count), 0)
    same = jnp.broadcast_to(owner_across, (count, count)) == jnp.broadcast_to(owner, (count, count))
    rank = jnp.sum(jnp.where(same & earlier, 1.0, 0.0), axis=1, keepdims=True)

    before = lax.rem(x + RING - 1, RING).astype(F32)
    here = x.astype(F32)
    after = lax.rem(x + 1, RING).astype(F32)
    across_ring = lax.rem(x + 2, RING).astype(F32)

    def owned(chip):
        return jnp.sum(jnp.where(owner == chip, 1.0, 0.0), axis=0, keepdims=True)

    own_before, own_here, own_after, own_across = owned(before), owned(here), owned(after), owned(across_ring)

    def upward(own, own_down, own_up):
        return jnp.minimum(jnp.maximum(jnp.floor(own * 0.5), own + own_down - cap), cap - own_up)

    up_before = upward(own_before, own_across, own_here)
    up_after = upward(own_after, own_here, own_across)
    up_across = upward(own_across, own_after, own_before)

    place = jnp.where(owner == here, row, 0.0)
    place = jnp.where(owner == before, 64.0 + rank, place)
    place = jnp.where(owner == after, 64.0 + cap + rank, place)
    width = 64 + 4 * cap

    def collect(skip_before, skip_after):
        far = jnp.where(
            rank < up_across,
            64.0 + 2 * cap + skip_before + rank,
            64.0 + 3 * cap + skip_after + rank - up_across,
        )
        source = jnp.where(owner == across_ring, far, place)
        return jnp.where(iota((count, width), 1) == source, 1.0, 0.0).astype(BF16)

    slot = iota((cap, 1), 0)
    rank_across, row_across = across(rank), across(row)
    hit = (jnp.broadcast_to(rank_across, (cap, count)) == iota((cap, count), 0)) & (
        jnp.broadcast_to(owner_across, (cap, count)) == here
    )
    own_row = jnp.sum(jnp.where(hit, jnp.broadcast_to(row_across, (cap, count)), 0.0), axis=1, keepdims=True)

    def forward(extra):
        return (
            jnp.where(extra < up_before, 64.0 + extra, -1.0),
            jnp.where(extra < own_after - up_after, 64.0 + cap + up_after + extra, -1.0),
        )

    def send(columns):
        source = jnp.concatenate(columns, axis=0)
        return jnp.where(iota((2 * cap, 64 + 2 * cap), 1) == source, 1.0, 0.0).astype(BF16)

    mixed = [jnp.where(slot < own_here, own_row, way) for way in forward(slot - own_here)]
    return (send(mixed), send(forward(slot))), (collect(own_before, own_after), collect(0.0, 0.0))


def gather_kernel(
    slots, chunks, width,
    snap_ref, picks_ref, rows_ref, sums_ref,
    picks, local, other, inbox, outbox, rows, send_hot, collect_hot, total, parts, gathered, sums,
    picks_sem, load_sem, swap_send, swap_recv, out_send, in_recv, pass_send, pass_recv, store_sem, sum_send, sum_recv,
):
    cap, head, tail = slots
    half = chunks * width
    snap, dof = lax.axis_index("snap"), lax.axis_index("dof")
    x, core = lax.div(snap, CORES), lax.rem(snap, CORES)
    sibling = (x * CORES + 1 - core, dof)
    up = (lax.rem(x + 1, RING) * CORES + core, dof)
    down = (lax.rem(x + RING - 1, RING) * CORES + core, dof)
    group = RING * RING
    others = [lax.rem(dof + k, group) for k in range(1, group)]
    peers = [sibling, up, down] + [(snap, peer) for peer in others]

    barrier = pltpu.get_barrier_semaphore()
    for peer in peers:
        pl.semaphore_signal(barrier, inc=1, device_id=peer, device_id_type=MESH)

    piece = half // PIECES
    mine = pl.multiple_of(core * half, half)
    theirs = pl.multiple_of((1 - core) * half, half)

    def load(index):
        start = pl.multiple_of(mine + index * piece, piece) if index < PIECES else theirs
        size = piece if index < PIECES else half
        where = (slice(None), pl.ds(start, size))
        return pltpu.make_async_copy(snap_ref.at[where], local.at[where], load_sem.at[index])

    def swap(index):
        start = pl.multiple_of(theirs + index * piece, piece)
        return pltpu.make_async_remote_copy(
            src_ref=snap_ref.at[:, pl.ds(start, piece)],
            dst_ref=other.at[:, pl.ds(index * piece, piece)],
            send_sem=swap_send.at[index],
            recv_sem=swap_recv.at[index],
            device_id=sibling,
            device_id_type=MESH,
        )

    load_picks = pltpu.make_async_copy(picks_ref, picks, picks_sem)
    load_picks.start()
    for index in range(PIECES + 1):
        load(index).start()
    total[...] = jnp.zeros_like(total)
    for way in range(2):
        for slot in range(LAG):
            inbox[way, slot] = jnp.zeros((cap, width), F32)
            if head < cap:
                inbox[way, LAG + slot, head:, :] = jnp.zeros((cap - head, width), F32)
            if tail < cap:
                inbox[way, LAG + chunks + slot, tail:, :] = jnp.zeros((cap - tail, width), F32)
    pl.semaphore_wait(barrier, len(peers))
    for index in range(PIECES):
        swap(index).start()
    load_picks.wait()
    send, collect = plan(picks[...].astype(F32), cap, x, core)
    for late in range(2):
        send_hot[late] = send[late]
        collect_hot[late] = collect[late]

    def message(step, way, size):
        return pltpu.make_async_remote_copy(
            src_ref=outbox.at[lax.rem(step, TX), way, pl.ds(0, size)],
            dst_ref=inbox.at[way, step + LAG, pl.ds(0, size)],
            send_sem=out_send.at[way, lax.rem(step, TX)],
            recv_sem=in_recv.at[way, lax.rem(step, SEMS)],
            device_id=up if way == 0 else down,
            device_id_type=MESH,
        )

    def messages(step, act):
        if head == cap and tail == cap:
            for way in range(2):
                act(message(step, way, cap))
            return
        for size, when in (
            (head, step < LAG),
            (cap, (step >= LAG) & (step < chunks)),
            (tail, step >= chunks),
        ):
            @pl.when(when)
            def _():
                for way in range(2):
                    act(message(step, way, size))

    def hand_over(chunk):
        return pltpu.make_async_remote_copy(
            src_ref=rows.at[core, chunk],
            dst_ref=rows.at[core, chunk],
            send_sem=pass_send.at[lax.rem(chunk, SEMS)],
            recv_sem=pass_recv.at[chunk],
            device_id=sibling,
            device_id_type=MESH,
        )

    def store(which, chunk, sem_row):
        return pltpu.make_async_copy(
            rows.at[which, chunk], rows_ref.at[which, chunk], store_sem.at[sem_row, lax.rem(chunk, SEMS)]
        )

    def local_chunk(base, chunk):
        return local[:, pl.ds(pl.multiple_of(base + chunk * width, width), width)]

    def other_chunk(chunk):
        return other[:, pl.ds(pl.multiple_of(chunk * width, width), width)]

    def add_products(which, picked, snaps):
        picked_parts, snap_parts = split(picked, 2), split(snaps, 2)
        stack = jnp.concatenate([picked_parts[0], snap_parts[0], picked_parts[1], snap_parts[1]], axis=0)
        total[which] += lax.dot_general(stack, stack, (((1,), (1,)), ((), ())), preferred_element_type=F32)

    def body(step, carry):
        for index in range(PIECES):
            @pl.when(step == index * (chunks // PIECES))
            def _():
                load(index).wait()
                swap(index).wait()

        @pl.when(step == LAG)
        def _():
            load(PIECES).wait()

        @pl.when((step >= LAG) & (step < chunks + 2 * LAG))
        def _():
            messages(step - LAG, lambda copy: copy.wait_recv())

        @pl.when(step < chunks + LAG)
        def _():
            @pl.when(step >= TX)
            def _():
                messages(step - TX, lambda copy: copy.wait_send())

            chunk = jnp.minimum(step, chunks - 1)
            stage = jnp.concatenate(
                [local_chunk(mine, chunk), other_chunk(chunk), inbox[0, step], inbox[1, step]], axis=0
            )
            sent = choose(send_hot[jnp.where(step < chunks, 0, 1)], stage)
            slot = lax.rem(step, TX)
            outbox[slot, 0] = sent[:cap]
            outbox[slot, 1] = sent[cap:]
            messages(step, lambda copy: copy.start())

        @pl.when((step >= 2 * LAG) & (step < chunks + 2 * LAG))
        def _():
            chunk = step - 2 * LAG
            here = local_chunk(mine, chunk)
            stage = jnp.concatenate(
                [here, other_chunk(chunk), inbox[0, step - LAG], inbox[1, step - LAG], inbox[0, step], inbox[1, step]],
                axis=0,
            )
            picked = choose(collect_hot[jnp.where(chunk < chunks - LAG, 0, 1)], stage)
            rows[core, chunk] = picked

            @pl.when(chunk >= SEMS)
            def _():
                hand_over(chunk - SEMS).wait_send()
                store(core, chunk - SEMS, 0).wait()

            hand_over(chunk).start()
            store(core, chunk, 0).start()
            add_products(core, picked, here)

        @pl.when(step >= 2 * LAG + 1)
        def _():
            chunk = step - 2 * LAG - 1
            hand_over(chunk).wait_recv()

            @pl.when(chunk >= SEMS)
            def _():
                store(1 - core, chunk - SEMS, 1).wait()

            store(1 - core, chunk, 1).start()
            add_products(1 - core, rows[1 - core, chunk], local_chunk(theirs, chunk))

        return carry

    lax.fori_loop(0, chunks + 2 * LAG + 1, body, 0)

    both = total[0] + total[1]
    wide = both.shape[0] // 2
    both = (both[:wide, :wide] + both[wide:, wide:]) + (both[:wide, wide:] + both[wide:, :wide])
    share = wide // group
    for index in range(group):
        parts[index] = both[index * share : (index + 1) * share]

    def give(k):
        return pltpu.make_async_remote_copy(
            src_ref=parts.at[others[k]],
            dst_ref=gathered.at[dof],
            send_sem=sum_send.at[0, k],
            recv_sem=sum_recv.at[0, k],
            device_id=(snap, others[k]),
            device_id_type=MESH,
        )

    def tell(k):
        return pltpu.make_async_remote_copy(
            src_ref=sums.at[dof],
            dst_ref=sums.at[dof],
            send_sem=sum_send.at[1, k],
            recv_sem=sum_recv.at[1, k],
            device_id=(snap, others[k]),
            device_id_type=MESH,
        )

    for k in range(group - 1):
        give(k).start()
    gathered[dof] = parts[dof]
    for k in range(group - 1):
        give(k).wait_recv()
    terms = [gathered[index] for index in range(group)]
    while len(terms) > 1:
        terms = [terms[i] + terms[i + 1] for i in range(0, len(terms), 2)]
    sums[dof] = terms[0] * (1.0 / (2 * half * group))
    for k in range(group - 1):
        tell(k).start()
    for k in range(group - 1):
        give(k).wait_send()
    for k in range(group - 1):
        tell(k).wait()
    for index in range(sums_ref.shape[0] // share):
        sums_ref[index * share : (index + 1) * share, :] = sums[index]

    for step in range(chunks + LAG - TX, chunks + LAG):
        for way in range(2):
            message(step, way, cap if step < chunks else tail).wait_send()
    for chunk in range(chunks - SEMS, chunks):
        hand_over(chunk).wait_send()
        store(core, chunk, 0).wait()
        store(1 - core, chunk, 1).wait()


def gather(snapshots, picks, slots, chunks, collective_id):
    cap = slots[0]
    snap_rows, cols = snapshots.shape
    steps, block = picks.shape
    snapshots = pltpu.with_memory_space_constraint(snapshots, pltpu.HBM)
    picks = pltpu.with_memory_space_constraint(picks, pltpu.HBM)
    count = steps * block
    half = cols // 2
    width = half // chunks
    wide = count + snap_rows
    group = RING * RING
    dma = pltpu.SemaphoreType.DMA
    return pl.pallas_call(
        functools.partial(gather_kernel, slots, chunks, width),
        name=f"gather_{cap}",
        out_shape=(
            jax.ShapeDtypeStruct((2, chunks, count, width), F32),
            jax.ShapeDtypeStruct((count, count + snap_rows), F32),
        ),
        in_specs=[pl.BlockSpec(memory_space=pl.ANY), pl.BlockSpec(memory_space=pl.ANY)],
        out_specs=(pl.BlockSpec(memory_space=pl.ANY), pl.BlockSpec(memory_space=pltpu.VMEM)),
        scratch_shapes=[
            pltpu.VMEM((steps, block), jnp.int32),
            pltpu.VMEM((snap_rows, cols), F32),
            pltpu.VMEM((snap_rows, half), F32),
            pltpu.VMEM((2, chunks + 2 * LAG, cap, width), F32),
            pltpu.VMEM((TX, 2, cap, width), F32),
            pltpu.VMEM((2, chunks, count, width), F32),
            pltpu.VMEM((2, 2 * cap, 64 + 2 * cap), BF16),
            pltpu.VMEM((2, count, 64 + 4 * cap), BF16),
            pltpu.VMEM((2, 2 * wide, 2 * wide), F32),
            pltpu.VMEM((group, wide // group, wide), F32),
            pltpu.VMEM((group, wide // group, wide), F32),
            pltpu.VMEM((group, wide // group, wide), F32),
            dma,
            dma((PIECES + 1,)),
            dma((PIECES,)),
            dma((PIECES,)),
            dma((2, TX)),
            dma((2, SEMS)),
            dma((SEMS,)),
            dma((chunks,)),
            dma((2, SEMS)),
            dma((2, group - 1)),
            dma((2, group - 1)),
        ],
        compiler_params=pltpu.CompilerParams(
            collective_id=collective_id, has_side_effects=True, vmem_limit_bytes=48 << 20
        ),
    )(snapshots, picks)


def eliminate(sums, count):
    tiles = count // 8
    lanes = sums.shape[1]
    shape = (8, lanes)
    left = [sums[8 * t : 8 * t + 8, :] for t in range(tiles)]
    right = [jnp.where(iota(shape, 1) == iota(shape, 0) + 8.0 * t, 1.0, 0.0) for t in range(tiles)]
    sub = iota(shape, 0)
    pivots = []

    def spread_row(tile, k):
        return jnp.broadcast_to(tile[k : k + 1, :], shape)

    def stack(values):
        out = values[0]
        for k in range(1, 8):
            out = jnp.where(sub == k, values[k], out)
        return out

    for b in range(tiles):
        columns = {
            t: [jnp.broadcast_to(left[t][:, 8 * b + k : 8 * b + k + 1], shape) for k in range(8)]
            for t in range(b, tiles)
        }
        left_rows = [spread_row(left[b], k) for k in range(8)]
        right_rows = [spread_row(right[b], k) for k in range(8)]
        corner = [[spread_row(columns[b][k], i) for k in range(i + 1)] for i in range(8)]
        inverse = []
        for k in range(8):
            inverse.append(1.0 / corner[k][k])
            factor = [None] * (k + 1) + [corner[i][k] * inverse[k] for i in range(k + 1, 8)]
            for i in range(k + 1, 8):
                for j in range(k + 1, i + 1):
                    corner[i][j] = corner[i][j] - factor[i] * corner[j][k]
            for i in range(k + 1, 8):
                left_rows[i] = left_rows[i] - factor[i] * left_rows[k]
                right_rows[i] = right_rows[i] - factor[i] * right_rows[k]
        left[b] = stack(left_rows)
        right[b] = stack(right_rows)
        pivots.append(stack([corner[k][k] for k in range(8)]))
        for t in range(b + 1, tiles):
            for k in range(8):
                factor = columns[t][k] * inverse[k]
                for later in range(k + 1, 8):
                    columns[t][later] = columns[t][later] - factor * corner[later][k]
                left[t] = left[t] - factor * left_rows[k]
                right[t] = right[t] - factor * right_rows[k]
    return jnp.concatenate(left, axis=0), jnp.concatenate(right, axis=0), jnp.concatenate(pivots, axis=0)


def apply_kernel(
    chunks, width, rows_ref, sums_ref, snap_ref, basis_ref, residual_ref,
    snaps, basis, residual, weights, snap_sem, basis_sem, residual_sem,
):
    count = basis.shape[0]
    load_snaps = pltpu.make_async_copy(snap_ref, snaps, snap_sem)
    load_snaps.start()

    left, right, pivots = eliminate(sums_ref[...], count)
    inverse = right[:, :count]
    cross = left[:, count:]
    scale = lax.rsqrt(pivots[:, :1])
    to_basis = inverse * scale
    coefficients = cross * (1.0 / pivots[:, : cross.shape[1]])
    to_residual = lax.dot_general(
        coefficients, inverse, (((0,), (0,)), ((), ())),
        precision=lax.Precision.HIGHEST, preferred_element_type=F32,
    )
    high, low = split(jnp.concatenate([to_basis, to_residual], axis=0), 2)
    weights[...] = jnp.concatenate([high, high, low], axis=1)

    def columns(index):
        return (slice(None), pl.ds(pl.multiple_of(index * width, width), width))

    def put(source, target, sem, index):
        wide = (slice(None), pl.ds(pl.multiple_of(index * (UNROLL * width), UNROLL * width), UNROLL * width))
        return pltpu.make_async_copy(source.at[wide], target.at[wide], sem.at[lax.rem(index, SEMS)])

    def put_basis(index):
        return put(basis, basis_ref, basis_sem, index)

    def put_residual(index):
        return put(residual, residual_ref, residual_sem, index)

    load_snaps.wait()
    steps = 2 * chunks // UNROLL

    def body(step, carry):
        for k in range(UNROLL):
            index = step * UNROLL + k
            high, low = split(rows_ref[index], 2)
            stack = jnp.concatenate([high, low, high], axis=0)
            out = jnp.dot(weights[...], stack, preferred_element_type=F32)
            where = columns(index)
            basis[where] = out[:count]
            residual[where] = snaps[where] - out[count:]

        put_basis(step).start()
        put_residual(step).start()
        return carry

    lax.fori_loop(0, steps, body, 0)
    for step in range(steps):
        put_basis(step).wait()
        put_residual(step).wait()


def apply(rows, sums, snapshots, chunks):
    snap_rows, cols = snapshots.shape
    snapshots = pltpu.with_memory_space_constraint(snapshots, pltpu.HBM)
    rows = pltpu.with_memory_space_constraint(rows, pltpu.VMEM)
    count = sums.shape[0]
    width = cols // (2 * chunks)
    dma = pltpu.SemaphoreType.DMA
    anywhere = pl.BlockSpec(memory_space=pl.ANY)
    return pl.pallas_call(
        functools.partial(apply_kernel, chunks, width),
        name="apply",
        out_shape=(jax.ShapeDtypeStruct((count, cols), F32), jax.ShapeDtypeStruct((snap_rows, cols), F32)),
        in_specs=[pl.BlockSpec(memory_space=pltpu.VMEM), pl.BlockSpec(memory_space=pltpu.VMEM), anywhere],
        out_specs=(anywhere, anywhere),
        scratch_shapes=[
            pltpu.VMEM((snap_rows, cols), F32),
            pltpu.VMEM((count, cols), F32),
            pltpu.VMEM((snap_rows, cols), F32),
            pltpu.VMEM((count + snap_rows, 3 * count), BF16),
            dma,
            dma((SEMS,)),
            dma((SEMS,)),
        ],
        compiler_params=pltpu.CompilerParams(vmem_limit_bytes=36 << 20),
    )(rows, sums, snapshots)


def on_device(snapshots, picks):
    chunks = CHUNKS
    counts = jnp.sum(1 << (8 * (picks // CHIP_ROWS)))
    owned = [(counts >> (8 * chip)) & 255 for chip in range(RING)]
    most = functools.reduce(jnp.maximum, owned)
    least = functools.reduce(jnp.minimum, owned)
    cap, head, _ = SMALL
    small = (most <= head) & (picks.size - least <= 2 * cap)
    rows, sums = lax.cond(
        small,
        lambda s, p: gather(s, p, SMALL, chunks, 0),
        lambda s, p: gather(s, p, LARGE, chunks, 1),
        snapshots,
        picks,
    )
    rows = rows.reshape((2 * chunks,) + rows.shape[2:])
    return apply(rows, sums, snapshots, chunks)


def solution(mesh):
    in_specs = (P("snap", "dof"), P())
    out_specs = (P(None, "dof"), P("snap", "dof"))
    return jax.shard_map(
        on_device, mesh=mesh, in_specs=in_specs, out_specs=out_specs, check_vma=False
    )
```

```python
import functools

import jax
import jax.numpy as jnp
from jax import lax
from jax.experimental import pallas as pl
from jax.experimental.pallas import tpu as pltpu
from jax.sharding import PartitionSpec as P

F32 = jnp.float32
BF16 = jnp.bfloat16
MESH = pl.DeviceIdType.MESH
RING = 4
CORES = 2
PIECES = 4
LAG = 3
TX = 6
SEMS = 16
CHIP_ROWS = 64
CHUNKS = 32
SMALL = (40, 32, 24)
LARGE = (48, 48, 48)
UNROLL = 8
PUT = 4


def iota(shape, dim):
    return lax.broadcasted_iota(jnp.int32, shape, dim).astype(F32)


def split(value, parts):
    out = []
    for index in range(parts):
        part = value.astype(BF16)
        out.append(part)
        if index < parts - 1:
            value = value - part.astype(F32)
    return out


def choose(one_hot, rows):
    total = None
    for part in split(rows, 3):
        term = jnp.dot(one_hot, part, preferred_element_type=F32)
        total = term if total is None else total + term
    return total


def plan(picks, cap, x, core):
    steps, block = picks.shape
    count = steps * block
    eye = iota((block, block), 0) == iota((block, block), 1)
    columns = [
        jnp.sum(jnp.where(eye, jnp.broadcast_to(picks[t : t + 1, :], (block, block)), 0.0), axis=1, keepdims=True)
        for t in range(steps)
    ]
    pick = jnp.concatenate(columns, axis=0)
    owner = jnp.floor(pick * (1.0 / CHIP_ROWS))
    row = pick - owner * CHIP_ROWS
    row = jnp.where(row < 32.0, row + 32.0 * core, row - 32.0 * core)
    big_eye = iota((count, count), 0) == iota((count, count), 1)

    def across(column):
        return jnp.sum(jnp.where(big_eye, jnp.broadcast_to(column, (count, count)), 0.0), axis=0, keepdims=True)

    owner_across = across(owner)
    earlier = iota((count, count), 1) < iota((count, count), 0)
    same = jnp.broadcast_to(owner_across, (count, count)) == jnp.broadcast_to(owner, (count, count))
    rank = jnp.sum(jnp.where(same & earlier, 1.0, 0.0), axis=1, keepdims=True)

    before = lax.rem(x + RING - 1, RING).astype(F32)
    here = x.astype(F32)
    after = lax.rem(x + 1, RING).astype(F32)
    across_ring = lax.rem(x + 2, RING).astype(F32)

    def owned(chip):
        return jnp.sum(jnp.where(owner == chip, 1.0, 0.0), axis=0, keepdims=True)

    own_before, own_here, own_after, own_across = owned(before), owned(here), owned(after), owned(across_ring)

    def upward(own, own_down, own_up):
        return jnp.minimum(jnp.maximum(jnp.floor(own * 0.5), own + own_down - cap), cap - own_up)

    up_before = upward(own_before, own_across, own_here)
    up_after = upward(own_after, own_here, own_across)
    up_across = upward(own_across, own_after, own_before)

    place = jnp.where(owner == here, row, 0.0)
    place = jnp.where(owner == before, 64.0 + rank, place)
    place = jnp.where(owner == after, 64.0 + cap + rank, place)
    width = 64 + 4 * cap

    def collect(skip_before, skip_after):
        far = jnp.where(
            rank < up_across,
            64.0 + 2 * cap + skip_before + rank,
            64.0 + 3 * cap + skip_after + rank - up_across,
        )
        source = jnp.where(owner == across_ring, far, place)
        return jnp.where(iota((count, width), 1) == source, 1.0, 0.0).astype(BF16)

    slot = iota((cap, 1), 0)
    rank_across, row_across = across(rank), across(row)
    hit = (jnp.broadcast_to(rank_across, (cap, count)) == iota((cap, count), 0)) & (
        jnp.broadcast_to(owner_across, (cap, count)) == here
    )
    own_row = jnp.sum(jnp.where(hit, jnp.broadcast_to(row_across, (cap, count)), 0.0), axis=1, keepdims=True)

    def forward(extra):
        return (
            jnp.where(extra < up_before, 64.0 + extra, -1.0),
            jnp.where(extra < own_after - up_after, 64.0 + cap + up_after + extra, -1.0),
        )

    def send(columns):
        source = jnp.concatenate(columns, axis=0)
        return jnp.where(iota((2 * cap, 64 + 2 * cap), 1) == source, 1.0, 0.0).astype(BF16)

    mixed = [jnp.where(slot < own_here, own_row, way) for way in forward(slot - own_here)]
    return (send(mixed), send(forward(slot))), (collect(own_before, own_after), collect(0.0, 0.0))


def gather_kernel(
    slots, chunks, width,
    snap_ref, picks_ref, rows_ref, sums_ref,
    picks, local, other, inbox, outbox, rows, send_hot, collect_hot, total, parts, gathered, sums,
    picks_sem, load_sem, swap_send, swap_recv, out_send, in_recv, pass_send, pass_recv, store_sem, sum_send, sum_recv,
):
    cap, head, tail = slots
    half = chunks * width
    snap, dof = lax.axis_index("snap"), lax.axis_index("dof")
    x, core = lax.div(snap, CORES), lax.rem(snap, CORES)
    sibling = (x * CORES + 1 - core, dof)
    up = (lax.rem(x + 1, RING) * CORES + core, dof)
    down = (lax.rem(x + RING - 1, RING) * CORES + core, dof)
    group = RING * RING
    others = [lax.rem(dof + k, group) for k in range(1, group)]
    peers = [sibling, up, down] + [(snap, peer) for peer in others]

    barrier = pltpu.get_barrier_semaphore()
    for peer in peers:
        pl.semaphore_signal(barrier, inc=1, device_id=peer, device_id_type=MESH)

    piece = half // PIECES
    mine = pl.multiple_of(core * half, half)
    theirs = pl.multiple_of((1 - core) * half, half)

    def load(index):
        start = pl.multiple_of(mine + index * piece, piece) if index < PIECES else theirs
        size = piece if index < PIECES else half
        where = (slice(None), pl.ds(start, size))
        return pltpu.make_async_copy(snap_ref.at[where], local.at[where], load_sem.at[index])

    def swap(index):
        start = pl.multiple_of(theirs + index * piece, piece)
        return pltpu.make_async_remote_copy(
            src_ref=snap_ref.at[:, pl.ds(start, piece)],
            dst_ref=other.at[:, pl.ds(index * piece, piece)],
            send_sem=swap_send.at[index],
            recv_sem=swap_recv.at[index],
            device_id=sibling,
            device_id_type=MESH,
        )

    load_picks = pltpu.make_async_copy(picks_ref, picks, picks_sem)
    load_picks.start()
    for index in range(PIECES + 1):
        load(index).start()
    total[...] = jnp.zeros_like(total)
    for way in range(2):
        for slot in range(LAG):
            inbox[way, slot] = jnp.zeros((cap, width), F32)
            if head < cap:
                inbox[way, LAG + slot, head:, :] = jnp.zeros((cap - head, width), F32)
            if tail < cap:
                inbox[way, LAG + chunks + slot, tail:, :] = jnp.zeros((cap - tail, width), F32)
    pl.semaphore_wait(barrier, len(peers))
    for index in range(PIECES):
        swap(index).start()
    load_picks.wait()
    send, collect = plan(picks[...].astype(F32), cap, x, core)
    for late in range(2):
        send_hot[late] = send[late]
        collect_hot[late] = collect[late]

    def message(step, way, size):
        return pltpu.make_async_remote_copy(
            src_ref=outbox.at[lax.rem(step, TX), way, pl.ds(0, size)],
            dst_ref=inbox.at[way, step + LAG, pl.ds(0, size)],
            send_sem=out_send.at[way, lax.rem(step, TX)],
            recv_sem=in_recv.at[way, lax.rem(step, SEMS)],
            device_id=up if way == 0 else down,
            device_id_type=MESH,
        )

    def messages(step, act):
        if head == cap and tail == cap:
            for way in range(2):
                act(message(step, way, cap))
            return
        for size, when in (
            (head, step < LAG),
            (cap, (step >= LAG) & (step < chunks)),
            (tail, step >= chunks),
        ):
            @pl.when(when)
            def _():
                for way in range(2):
                    act(message(step, way, size))

    def hand_over(chunk):
        return pltpu.make_async_remote_copy(
            src_ref=rows.at[core, chunk],
            dst_ref=rows.at[core, chunk],
            send_sem=pass_send.at[lax.rem(chunk, SEMS)],
            recv_sem=pass_recv.at[chunk],
            device_id=sibling,
            device_id_type=MESH,
        )

    def store(which, chunk, sem_row):
        return pltpu.make_async_copy(
            rows.at[which, chunk], rows_ref.at[which, chunk], store_sem.at[sem_row, lax.rem(chunk, SEMS)]
        )

    def local_chunk(base, chunk):
        return local[:, pl.ds(pl.multiple_of(base + chunk * width, width), width)]

    def other_chunk(chunk):
        return other[:, pl.ds(pl.multiple_of(chunk * width, width), width)]

    def add_products(which, picked, snaps):
        picked_parts, snap_parts = split(picked, 2), split(snaps, 2)
        stack = jnp.concatenate([picked_parts[0], snap_parts[0], picked_parts[1], snap_parts[1]], axis=0)
        total[which] += lax.dot_general(stack, stack, (((1,), (1,)), ((), ())), preferred_element_type=F32)

    def body(step, carry):
        for index in range(PIECES):
            @pl.when(step == index * (chunks // PIECES))
            def _():
                load(index).wait()
                swap(index).wait()

        @pl.when(step == LAG)
        def _():
            load(PIECES).wait()

        @pl.when((step >= LAG) & (step < chunks + 2 * LAG))
        def _():
            messages(step - LAG, lambda copy: copy.wait_recv())

        @pl.when(step < chunks + LAG)
        def _():
            @pl.when(step >= TX)
            def _():
                messages(step - TX, lambda copy: copy.wait_send())

            chunk = jnp.minimum(step, chunks - 1)
            stage = jnp.concatenate(
                [local_chunk(mine, chunk), other_chunk(chunk), inbox[0, step], inbox[1, step]], axis=0
            )
            sent = choose(send_hot[jnp.where(step < chunks, 0, 1)], stage)
            slot = lax.rem(step, TX)
            outbox[slot, 0] = sent[:cap]
            outbox[slot, 1] = sent[cap:]
            messages(step, lambda copy: copy.start())

        @pl.when((step >= 2 * LAG) & (step < chunks + 2 * LAG))
        def _():
            chunk = step - 2 * LAG
            here = local_chunk(mine, chunk)
            stage = jnp.concatenate(
                [here, other_chunk(chunk), inbox[0, step - LAG], inbox[1, step - LAG], inbox[0, step], inbox[1, step]],
                axis=0,
            )
            picked = choose(collect_hot[jnp.where(chunk < chunks - LAG, 0, 1)], stage)
            rows[core, chunk] = picked

            @pl.when(chunk >= SEMS)
            def _():
                hand_over(chunk - SEMS).wait_send()
                store(core, chunk - SEMS, 0).wait()

            hand_over(chunk).start()
            store(core, chunk, 0).start()
            add_products(core, picked, here)

        @pl.when(step >= 2 * LAG + 1)
        def _():
            chunk = step - 2 * LAG - 1
            hand_over(chunk).wait_recv()

            @pl.when(chunk >= SEMS)
            def _():
                store(1 - core, chunk - SEMS, 1).wait()

            store(1 - core, chunk, 1).start()
            add_products(1 - core, rows[1 - core, chunk], local_chunk(theirs, chunk))

        return carry

    lax.fori_loop(0, chunks + 2 * LAG + 1, body, 0)

    both = total[0] + total[1]
    wide = both.shape[0] // 2
    both = (both[:wide, :wide] + both[wide:, wide:]) + (both[:wide, wide:] + both[wide:, :wide])
    share = wide // group
    for index in range(group):
        parts[index] = both[index * share : (index + 1) * share]

    def give(k):
        return pltpu.make_async_remote_copy(
            src_ref=parts.at[others[k]],
            dst_ref=gathered.at[dof],
            send_sem=sum_send.at[0, k],
            recv_sem=sum_recv.at[0, k],
            device_id=(snap, others[k]),
            device_id_type=MESH,
        )

    def tell(k):
        return pltpu.make_async_remote_copy(
            src_ref=sums.at[dof],
            dst_ref=sums.at[dof],
            send_sem=sum_send.at[1, k],
            recv_sem=sum_recv.at[1, k],
            device_id=(snap, others[k]),
            device_id_type=MESH,
        )

    for k in range(group - 1):
        give(k).start()
    gathered[dof] = parts[dof]
    for k in range(group - 1):
        give(k).wait_recv()
    terms = [gathered[index] for index in range(group)]
    while len(terms) > 1:
        terms = [terms[i] + terms[i + 1] for i in range(0, len(terms), 2)]
    sums[dof] = terms[0] * (1.0 / (2 * half * group))
    for k in range(group - 1):
        tell(k).start()
    for k in range(group - 1):
        give(k).wait_send()
    for k in range(group - 1):
        tell(k).wait()
    for index in range(sums_ref.shape[0] // share):
        sums_ref[index * share : (index + 1) * share, :] = sums[index]

    for step in range(chunks + LAG - TX, chunks + LAG):
        for way in range(2):
            message(step, way, cap if step < chunks else tail).wait_send()
    for chunk in range(chunks - SEMS, chunks):
        hand_over(chunk).wait_send()
        store(core, chunk, 0).wait()
        store(1 - core, chunk, 1).wait()


def gather(snapshots, picks, slots, chunks, collective_id):
    cap = slots[0]
    snap_rows, cols = snapshots.shape
    steps, block = picks.shape
    snapshots = pltpu.with_memory_space_constraint(snapshots, pltpu.HBM)
    picks = pltpu.with_memory_space_constraint(picks, pltpu.HBM)
    count = steps * block
    half = cols // 2
    width = half // chunks
    wide = count + snap_rows
    group = RING * RING
    dma = pltpu.SemaphoreType.DMA
    return pl.pallas_call(
        functools.partial(gather_kernel, slots, chunks, width),
        name=f"gather_{cap}",
        out_shape=(
            jax.ShapeDtypeStruct((2, chunks, count, width), F32),
            jax.ShapeDtypeStruct((count, count + snap_rows), F32),
        ),
        in_specs=[pl.BlockSpec(memory_space=pl.ANY), pl.BlockSpec(memory_space=pl.ANY)],
        out_specs=(pl.BlockSpec(memory_space=pl.ANY), pl.BlockSpec(memory_space=pltpu.VMEM)),
        scratch_shapes=[
            pltpu.VMEM((steps, block), jnp.int32),
            pltpu.VMEM((snap_rows, cols), F32),
            pltpu.VMEM((snap_rows, half), F32),
            pltpu.VMEM((2, chunks + 2 * LAG, cap, width), F32),
            pltpu.VMEM((TX, 2, cap, width), F32),
            pltpu.VMEM((2, chunks, count, width), F32),
            pltpu.VMEM((2, 2 * cap, 64 + 2 * cap), BF16),
            pltpu.VMEM((2, count, 64 + 4 * cap), BF16),
            pltpu.VMEM((2, 2 * wide, 2 * wide), F32),
            pltpu.VMEM((group, wide // group, wide), F32),
            pltpu.VMEM((group, wide // group, wide), F32),
            pltpu.VMEM((group, wide // group, wide), F32),
            dma,
            dma((PIECES + 1,)),
            dma((PIECES,)),
            dma((PIECES,)),
            dma((2, TX)),
            dma((2, SEMS)),
            dma((SEMS,)),
            dma((chunks,)),
            dma((2, SEMS)),
            dma((2, group - 1)),
            dma((2, group - 1)),
        ],
        compiler_params=pltpu.CompilerParams(
            collective_id=collective_id, has_side_effects=True, vmem_limit_bytes=48 << 20
        ),
    )(snapshots, picks)


def eliminate(sums, count):
    tiles = count // 8
    lanes = sums.shape[1]
    shape = (8, lanes)
    left = [sums[8 * t : 8 * t + 8, :] for t in range(tiles)]
    right = [jnp.where(iota(shape, 1) == iota(shape, 0) + 8.0 * t, 1.0, 0.0) for t in range(tiles)]
    sub = iota(shape, 0)
    pivots = []

    def spread_row(tile, k):
        return jnp.broadcast_to(tile[k : k + 1, :], shape)

    def stack(values):
        out = values[0]
        for k in range(1, 8):
            out = jnp.where(sub == k, values[k], out)
        return out

    for b in range(tiles):
        columns = {
            t: [jnp.broadcast_to(left[t][:, 8 * b + k : 8 * b + k + 1], shape) for k in range(8)]
            for t in range(b, tiles)
        }
        left_rows = [spread_row(left[b], k) for k in range(8)]
        right_rows = [spread_row(right[b], k) for k in range(8)]
        corner = [[spread_row(columns[b][k], i) for k in range(i + 1)] for i in range(8)]
        inverse = []
        for k in range(8):
            inverse.append(1.0 / corner[k][k])
            factor = [None] * (k + 1) + [corner[i][k] * inverse[k] for i in range(k + 1, 8)]
            for i in range(k + 1, 8):
                for j in range(k + 1, i + 1):
                    corner[i][j] = corner[i][j] - factor[i] * corner[j][k]
            for i in range(k + 1, 8):
                left_rows[i] = left_rows[i] - factor[i] * left_rows[k]
                right_rows[i] = right_rows[i] - factor[i] * right_rows[k]
        left[b] = stack(left_rows)
        right[b] = stack(right_rows)
        pivots.append(stack([corner[k][k] for k in range(8)]))
        for t in range(b + 1, tiles):
            for k in range(8):
                factor = columns[t][k] * inverse[k]
                for later in range(k + 1, 8):
                    columns[t][later] = columns[t][later] - factor * corner[later][k]
                left[t] = left[t] - factor * left_rows[k]
                right[t] = right[t] - factor * right_rows[k]
    return jnp.concatenate(left, axis=0), jnp.concatenate(right, axis=0), jnp.concatenate(pivots, axis=0)


def apply_kernel(
    chunks, width, rows_ref, sums_ref, snap_ref, basis_ref, residual_ref,
    snaps, basis, residual, weights, snap_sem, basis_sem, residual_sem,
):
    count = basis.shape[0]
    load_snaps = pltpu.make_async_copy(snap_ref, snaps, snap_sem)
    load_snaps.start()

    left, right, pivots = eliminate(sums_ref[...], count)
    inverse = right[:, :count]
    cross = left[:, count:]
    scale = lax.rsqrt(pivots[:, :1])
    to_basis = inverse * scale
    coefficients = cross * (1.0 / pivots[:, : cross.shape[1]])
    to_residual = lax.dot_general(
        coefficients, inverse, (((0,), (0,)), ((), ())),
        precision=lax.Precision.HIGHEST, preferred_element_type=F32,
    )
    high, low = split(jnp.concatenate([to_basis, to_residual], axis=0), 2)
    weights[...] = jnp.concatenate([high, high, low], axis=1)

    def columns(index):
        return (slice(None), pl.ds(pl.multiple_of(index * width, width), width))

    def put(source, target, sem, index):
        wide = (slice(None), pl.ds(pl.multiple_of(index * (PUT * width), PUT * width), PUT * width))
        return pltpu.make_async_copy(source.at[wide], target.at[wide], sem.at[lax.rem(index, SEMS)])

    def put_basis(index):
        return put(basis, basis_ref, basis_sem, index)

    def put_residual(index):
        return put(residual, residual_ref, residual_sem, index)

    load_snaps.wait()
    steps = 2 * chunks // UNROLL

    def body(step, carry):
        for k in range(UNROLL):
            index = step * UNROLL + k
            high, low = split(rows_ref[index], 2)
            stack = jnp.concatenate([high, low, high], axis=0)
            out = jnp.dot(weights[...], stack, preferred_element_type=F32)
            where = columns(index)
            basis[where] = out[:count]
            residual[where] = snaps[where] - out[count:]

            if k % PUT == PUT - 1:
                put_basis(step * (UNROLL // PUT) + k // PUT).start()
                put_residual(step * (UNROLL // PUT) + k // PUT).start()

        return carry

    lax.fori_loop(0, steps, body, 0)
    for index in range(2 * chunks // PUT):
        put_basis(index).wait()
        put_residual(index).wait()


def apply(rows, sums, snapshots, chunks):
    snap_rows, cols = snapshots.shape
    snapshots = pltpu.with_memory_space_constraint(snapshots, pltpu.HBM)
    rows = pltpu.with_memory_space_constraint(rows, pltpu.VMEM)
    count = sums.shape[0]
    width = cols // (2 * chunks)
    dma = pltpu.SemaphoreType.DMA
    anywhere = pl.BlockSpec(memory_space=pl.ANY)
    return pl.pallas_call(
        functools.partial(apply_kernel, chunks, width),
        name="apply",
        out_shape=(jax.ShapeDtypeStruct((count, cols), F32), jax.ShapeDtypeStruct((snap_rows, cols), F32)),
        in_specs=[pl.BlockSpec(memory_space=pltpu.VMEM), pl.BlockSpec(memory_space=pltpu.VMEM), anywhere],
        out_specs=(anywhere, anywhere),
        scratch_shapes=[
            pltpu.VMEM((snap_rows, cols), F32),
            pltpu.VMEM((count, cols), F32),
            pltpu.VMEM((snap_rows, cols), F32),
            pltpu.VMEM((count + snap_rows, 3 * count), BF16),
            dma,
            dma((SEMS,)),
            dma((SEMS,)),
        ],
        compiler_params=pltpu.CompilerParams(vmem_limit_bytes=36 << 20),
    )(rows, sums, snapshots)


def on_device(snapshots, picks):
    chunks = CHUNKS
    counts = jnp.sum(1 << (8 * (picks // CHIP_ROWS)))
    owned = [(counts >> (8 * chip)) & 255 for chip in range(RING)]
    most = functools.reduce(jnp.maximum, owned)
    least = functools.reduce(jnp.minimum, owned)
    cap, head, _ = SMALL
    small = (most <= head) & (picks.size - least <= 2 * cap)
    rows, sums = lax.cond(
        small,
        lambda s, p: gather(s, p, SMALL, chunks, 0),
        lambda s, p: gather(s, p, LARGE, chunks, 1),
        snapshots,
        picks,
    )
    rows = rows.reshape((2 * chunks,) + rows.shape[2:])
    return apply(rows, sums, snapshots, chunks)


def solution(mesh):
    in_specs = (P("snap", "dof"), P())
    out_specs = (P(None, "dof"), P("snap", "dof"))
    return jax.shard_map(
        on_device, mesh=mesh, in_specs=in_specs, out_specs=out_specs, check_vma=False
    )
```
